512 devices in a mesh: segment: 4 (over y_hi), tile: 16 (over z, y_lo), frame: 8 (over x, core).
Axes of the slice: x: 4, y: 8 (y_hi: 4, y_lo: 2; y = y_hi * 2 + y_lo), z: 8, core: 2. Of those that a mesh axis runs over, the one named last changes fastest.
Arguments:
- corrupted_clip: bfloat16 [4, 16, 128, 64, 128], P('segment', 'frame', 'tile'), may hold values from -6 to 6
- completed_clip_upsized: bfloat16 [4, 16, 128, 64, 128], P('segment', 'frame', 'tile'), may hold values from -6 to 6
- conditioning_frame: int32 [4, 16], P('segment', 'frame'), may hold values from 0 to 15
- inbound_kernel_matrix: bfloat16 [4, 3, 3, 256, 128], P('segment'), may hold values from -0.125 to 0.125
- skip_kernel_matrix: bfloat16 [4, 3, 3, 128, 128], P('segment'), may hold values from -0.1875 to 0.1875
- projection_matrices: bfloat16 [4, 4, 128, 128], P('segment'), may hold values from -0.5 to 0.5
- branch_logit_factor: float32 [4, 2], P('segment'), may hold values from 1 to 600
- expand_matrix: bfloat16 [4, 128, 512], P('segment'), may hold values from -0.5 to 0.5
- contract_matrix: bfloat16 [4, 512, 128], P('segment'), may hold values from -0.25 to 0.25
- outbound_kernel_matrix: bfloat16 [4, 3, 3, 128, 128], P('segment'), may hold values from -0.1875 to 0.1875
- update_factors: float32 [4, 2], P('segment'), may hold values from 0.2 to 1
Outputs:
- denoised_clip: bfloat16 [4, 16, 128, 64, 128], P('segment', 'frame', 'tile')
- predicted_perturbation: bfloat16 [4, 16, 128, 64, 128], P('segment', 'frame', 'tile')
The draws below stay inside these ranges and needn't reach their ends.
All inputs are finite; a program needn't handle non-finite values.
Results may differ from the reference program's by a relative error of at most 0.014.
Values may be sent and summed in bfloat16 or wider, within the bound.
A program may use at most 64 MiB of HBM per device.

```python
import jax
import jax.numpy as jnp
from jax import lax

C = 128
HEADS = 2
W = 64
SEGMENTS = 4
FRAMES = 16
H = 128


def draw_branch_logit_factor(key, part):
    key = jax.random.fold_in(key, 7)
    return jnp.exp(jax.random.uniform(key, (SEGMENTS, HEADS), jnp.float32, 0.0, jnp.log(8.0)))


def touch_ends(drawn, own_key, low, top_value):
    longest = drawn.shape.index(max(drawn.shape))
    spots = []
    for shift in (0, 1):
        where = [jax.random.randint(jax.random.fold_in(own_key, axis), (), 0, length) for axis, length in enumerate(drawn.shape)]
        where[longest] = (where[longest] + shift) % drawn.shape[longest]
        spots.append(tuple(where))
    return drawn.at[spots[0]].set(low).at[spots[1]].set(top_value)


def steps_of(key, shape, pieces, low, top_value):
    factor_of = 1.0
    for axis_at, blocks in pieces:
        heights = jax.random.uniform(jax.random.fold_in(jax.random.fold_in(key, 6), axis_at), (blocks,), jnp.float32, low / len(pieces), top_value / len(pieces))
        factor_of = factor_of * jnp.repeat(jnp.exp(heights), shape[axis_at] // blocks).reshape((-1,) + (1,) * (len(shape) - 1 - axis_at))
    return factor_of


def centred(key, shape, spread, reach, pieces=(), held_as=jnp.bfloat16):
    loudness = steps_of(key, shape, pieces, -0.22, 0.18) if pieces else 1.0
    array = jax.random.normal(key, shape, jnp.float32) * spread * loudness
    return jnp.minimum(jnp.maximum(array, -reach), reach).astype(held_as)


def setup_inputs(seed: int = 0) -> dict:
    keys = jax.random.split(jax.random.key(seed), 12)
    corrupted_clip = centred(keys[0], (SEGMENTS, FRAMES, H, W, C), 1.0, 6.0, ((0, 4), (1, 8), (2, 16)))
    completed_clip_upsized = centred(keys[1], (SEGMENTS, FRAMES, H, W, C), 1.0, 6.0, ((0, 4), (1, 8), (2, 16)))
    conditioning_frame = touch_ends(jax.random.randint(keys[2], (SEGMENTS, FRAMES), 0, FRAMES), jax.random.fold_in(keys[2], 1), 0, FRAMES - 1).astype(jnp.int32)
    inbound_kernel_matrix = centred(keys[3], (SEGMENTS, 3, 3, 2 * C, C), (18 * C) ** -0.5, 0.125, ((0, 4),))
    skip_kernel_matrix = centred(keys[4], (SEGMENTS, 3, 3, C, C), (9 * C) ** -0.5, 0.1875, ((0, 4),))
    projection_matrices = centred(keys[5], (SEGMENTS, 4, C, C), C ** -0.5, 0.5, ((0, 4),))
    branch_logit_factor = draw_branch_logit_factor(jax.random.fold_in(keys[11], 71), 0)
    expand_matrix = centred(keys[7], (SEGMENTS, C, 4 * C), C ** -0.5, 0.5, ((0, 4),))
    contract_matrix = centred(keys[8], (SEGMENTS, 4 * C, C), (4 * C) ** -0.5, 0.25, ((0, 4),))
    outbound_kernel_matrix = centred(keys[9], (SEGMENTS, 3, 3, C, C), (9 * C) ** -0.5, 0.1875, ((0, 4),))
    update_factors = jnp.clip(0.2 + 0.8 * jax.random.uniform(keys[10], (SEGMENTS, 2), jnp.float32) ** steps_of(keys[10], (SEGMENTS, 2), ((0, 4),), -0.2, 0.2), 0.2, 1.0)
    return {"corrupted_clip": corrupted_clip, "completed_clip_upsized": completed_clip_upsized, "conditioning_frame": conditioning_frame, "inbound_kernel_matrix": inbound_kernel_matrix, "skip_kernel_matrix": skip_kernel_matrix, "projection_matrices": projection_matrices, "branch_logit_factor": branch_logit_factor, "expand_matrix": expand_matrix, "contract_matrix": contract_matrix, "outbound_kernel_matrix": outbound_kernel_matrix, "update_factors": update_factors}


def conv(x, kernel):
    return lax.conv_general_dilated(x.astype(jnp.float32), kernel.astype(jnp.float32), (1, 1), 'SAME', dimension_numbers=('NHWC', 'HWIO', 'NHWC'), precision=lax.Precision.HIGHEST)

def rms(value):
    return value * lax.rsqrt(lax.optimization_barrier(jnp.mean(value * value, axis=-1, keepdims=True)) + 1e-06)

def cascade_position(inputs):
    corrupted_clip, conditioning_source, w_in, w_mid, proj, temp, w_up, w_down, w_out, coef = inputs
    frames, rows, width, chans = corrupted_clip.shape
    per_branch_width = chans // HEADS
    joined = jnp.concatenate([corrupted_clip, conditioning_source], axis=-1)
    h1 = jax.nn.silu(conv(joined, w_in)).astype(jnp.bfloat16)
    a = h1.astype(jnp.float32) + conv(h1, w_mid)
    u = rms(a).astype(jnp.bfloat16).astype(jnp.float32)
    pf = [p.astype(jnp.float32) for p in (proj[0], proj[1], proj[2], proj[3])]
    q = jnp.einsum('fxyc,cd->fxyd', u, pf[0]).reshape(frames, rows, width, HEADS, per_branch_width)
    k = jnp.einsum('fxyc,cd->fxyd', u, pf[1]).reshape(frames, rows, width, HEADS, per_branch_width)
    v = jnp.einsum('fxyc,cd->fxyd', u, pf[2]).astype(jnp.bfloat16).reshape(frames, rows, width, HEADS, per_branch_width)
    qn = rms(q).astype(jnp.bfloat16).astype(jnp.float32)
    kn = rms(k).astype(jnp.bfloat16).astype(jnp.float32)
    scores = jnp.einsum('fxyhd,gxyhd->fgxyh', qn, kn) * (temp / per_branch_width)
    peak = lax.optimization_barrier(jnp.max(scores, axis=1, keepdims=True))
    raw = jnp.exp(scores - peak)
    total = lax.optimization_barrier(jnp.sum(raw, axis=1))
    weights = raw.astype(jnp.bfloat16).astype(jnp.float32)
    acc = jnp.einsum('fgxyh,gxyhd->fxyhd', weights, v.astype(jnp.float32))
    o = (acc / total[..., None]).astype(jnp.bfloat16).reshape(frames, rows, width, chans)
    b = a + jnp.einsum('fxyc,cd->fxyd', o.astype(jnp.float32), pf[3])
    r = rms(b).astype(jnp.bfloat16).astype(jnp.float32)
    m = jax.nn.silu(jnp.einsum('fxyc,cd->fxyd', r, w_up.astype(jnp.float32))).astype(jnp.bfloat16)
    c = (b + jnp.einsum('fxyc,cd->fxyd', m.astype(jnp.float32), w_down.astype(jnp.float32))).astype(jnp.bfloat16)
    eps = conv(c, w_out)
    denoised_clip = coef[0] * corrupted_clip.astype(jnp.float32) - coef[1] * eps
    return (denoised_clip.astype(jnp.bfloat16), eps.astype(jnp.bfloat16))

def reference(corrupted_clip, completed_clip_upsized, conditioning_frame, inbound_kernel_matrix, skip_kernel_matrix, projection_matrices, branch_logit_factor, expand_matrix, contract_matrix, outbound_kernel_matrix, update_factors):
    previous = jnp.concatenate([jnp.zeros_like(completed_clip_upsized[:1]), completed_clip_upsized[:-1]], axis=0)
    conditioning_source = jax.vmap(lambda clip, picks: jnp.take(clip, picks, axis=0))(previous, conditioning_frame)
    denoised_clip, predicted_perturbation = lax.map(cascade_position, (corrupted_clip, conditioning_source, inbound_kernel_matrix, skip_kernel_matrix, projection_matrices, branch_logit_factor, expand_matrix, contract_matrix, outbound_kernel_matrix, update_factors))
    return (denoised_clip, predicted_perturbation)
```

```python
import functools

import jax
import jax.numpy as jnp
from jax import lax
from jax.experimental import pallas as pl
from jax.experimental.pallas import tpu as pltpu
from jax.sharding import PartitionSpec as P

MESH = pl.DeviceIdType.MESH
BF = jnp.bfloat16
F32 = jnp.float32
PR, PC, NF, CH = 4, 16, 16, 128
DIRS = [(-1, 0), (1, 0), (0, -1), (0, 1), (-1, -1), (-1, 1), (1, -1), (1, 1)]
SRC_ROWS = {-1: slice(1, 2), 1: slice(PR, PR + 1), 0: slice(1, PR + 1)}
DST_ROWS = {-1: slice(PR + 1, PR + 2), 1: slice(0, 1), 0: slice(1, PR + 1)}
SRC_COLS = {-1: slice(1, 2), 1: slice(PC, PC + 1), 0: slice(1, PC + 1)}
DST_COLS = {-1: slice(PC + 1, PC + 2), 1: slice(0, 1), 0: slice(1, PC + 1)}


def dot(a, b):
    return jnp.dot(a, b, preferred_element_type=F32)


def lane_sums(v, ones):
    hi = v.astype(BF)
    lo = (v - hi.astype(F32)).astype(BF)
    return dot(jnp.concatenate([hi, lo], axis=1), jnp.concatenate([ones, ones], axis=0))


def silu(v):
    return v / (1.0 + jnp.exp(-v))


def kernel(
    x_hbm, clip_hbm, picks, w_in, w_mid, proj, factors, w_up, w_dn, w_out, coefs,
    den_out, eps_out,
    raw_n, raw_c, xn, xc, hb, cb, acc, res, pk, send_e, eo, xv, dv,
    v_in_n, v_in_c, v_mid, v_qkv, v_o, v_up, v_dn, v_out,
    s_w, s_pk, r_pk, s_c, r_c, s_n, r_n, s_h, r_h, s_e, r_e, s_fin,
):
    s = lax.axis_index("segment")
    t = lax.axis_index("tile")
    d = lax.axis_index("frame")
    i, j = lax.rem(d, 2), lax.div(d, 2)
    big_row = 2 * t + i
    last_row = 2 * lax.axis_size("tile") - 1

    weights = [
        (w_in.at[0, :, :, 0:CH, :], v_in_n),
        (x_hbm.at[0], xv),
        (w_in.at[0, :, :, CH : 2 * CH, :], v_in_c),
        (w_mid.at[0], v_mid),
        (proj.at[0, 0], v_qkv.at[:, 0:CH]),
        (proj.at[0, 1], v_qkv.at[:, CH : 2 * CH]),
        (proj.at[0, 2], v_qkv.at[:, 2 * CH : 3 * CH]),
        (proj.at[0, 3], v_o),
        (w_up.at[0], v_up),
        (w_dn.at[0], v_dn),
        (w_out.at[0], v_out),
    ]
    loads = [pltpu.make_async_copy(a, b, s_w.at[q]) for q, (a, b) in enumerate(weights)]

    def neighbour(step_row, step_col):
        row = lax.rem(big_row + step_row + last_row + 1, last_row + 1)
        col = lax.rem(j + step_col + 4, 4)
        return {"tile": lax.div(row, 2), "frame": 2 * col + lax.rem(row, 2)}

    def in_group(k):
        return lax.rem(d + k, 8)

    barrier = pltpu.get_barrier_semaphore()
    for k in range(8):
        for step in (1, 3):
            pl.semaphore_signal(
                barrier, inc=1, device_id={"segment": lax.rem(s + step, 4), "frame": in_group(k)}, device_id_type=MESH
            )
    for k in range(1, 8):
        pl.semaphore_signal(barrier, inc=1, device_id={"frame": in_group(k)}, device_id_type=MESH)
    for step in DIRS:
        pl.semaphore_signal(barrier, inc=1, device_id=neighbour(*step), device_id_type=MESH)
    for load in loads:
        load.start()
    pl.semaphore_wait(barrier, 16 + 7 + 8)

    def patch_of(ref, c):
        return ref.at[0, :, pl.ds(PR * lax.rem(c, 2), PR), pl.ds(pl.multiple_of(PC * lax.div(c, 2), PC), PC), :]

    clip_copies = [
        pltpu.make_async_remote_copy(
            src_ref=patch_of(clip_hbm, in_group(k)),
            dst_ref=raw_c.at[d],
            send_sem=s_c.at[k],
            recv_sem=r_c.at[k],
            device_id={"segment": lax.rem(s + 1, 4), "frame": in_group(k)},
            device_id_type=MESH,
        )
        for k in range(8)
    ]

    @pl.when(s < 3)
    def _():
        for copy in clip_copies:
            copy.start()

    frame_row = lax.broadcasted_iota(jnp.int32, (NF, CH), 0)
    pk[d] = jnp.where(frame_row == 2 * d, picks[0, 0], jnp.where(frame_row == 2 * d + 1, picks[0, 1], 0)).astype(F32)
    pick_copies, noisy_copies = [], []
    own_noisy = pltpu.make_async_copy(patch_of(x_hbm, d), raw_n.at[d], s_n.at[0])
    own_noisy.start()
    for k in range(1, 8):
        noisy_copies.append(
            pltpu.make_async_remote_copy(
                src_ref=patch_of(x_hbm, in_group(k)),
                dst_ref=raw_n.at[d],
                send_sem=s_n.at[k],
                recv_sem=r_n.at[k],
                device_id={"frame": in_group(k)},
                device_id_type=MESH,
            )
        )
        noisy_copies[-1].start()
    for k in range(1, 8):
        pick_copies.append(
            pltpu.make_async_remote_copy(
                src_ref=pk.at[d],
                dst_ref=pk.at[d],
                send_sem=s_pk.at[k],
                recv_sem=r_pk.at[k],
                device_id={"frame": in_group(k)},
                device_id_type=MESH,
            )
        )
        pick_copies[-1].start()

    r_i = lax.broadcasted_iota(jnp.int32, (256, 256), 0)
    c_i = lax.broadcasted_iota(jnp.int32, (256, 256), 1)
    r_hi, r_lo, c_hi, c_lo = r_i // 16, r_i % 16, c_i // 16, c_i % 16
    swap = jnp.where((r_hi == c_lo) & (r_lo == c_hi), 1.0, 0.0).astype(BF)

    def halo_copies(buf, n):
        copies = []
        for k, (dr, dc) in enumerate(DIRS):
            copies.append(
                pltpu.make_async_remote_copy(
                    src_ref=buf.at[SRC_ROWS[dr], SRC_COLS[dc]],
                    dst_ref=buf.at[DST_ROWS[dr], DST_COLS[dc]],
                    send_sem=s_h.at[n, k],
                    recv_sem=r_h.at[n, k],
                    device_id=neighbour(dr, dc),
                    device_id_type=MESH,
                )
            )
        return copies

    def halo_end(buf, copies):
        for copy in copies:
            copy.wait_recv()

        @pl.when(big_row == 0)
        def _():
            buf[0] = jnp.zeros((PC + 2, NF, CH), BF)

        @pl.when(big_row == last_row)
        def _():
            buf[PR + 1] = jnp.zeros((PC + 2, NF, CH), BF)

        @pl.when(j == 0)
        def _():
            buf[:, 0:1] = jnp.zeros((PR + 2, 1, NF, CH), BF)

        @pl.when(j == 3)
        def _():
            buf[:, PC + 1 : PC + 2] = jnp.zeros((PR + 2, 1, NF, CH), BF)

    def conv(buf, w, row, rows):
        n = rows * PC * NF
        parts = [
            buf[row + dr : row + dr + rows, dc : dc + PC].reshape(n, CH) for dr in range(3) for dc in range(3)
        ]
        return dot(jnp.concatenate(parts, axis=1), w[...].reshape(9 * CH, w.shape[3]))

    own_noisy.wait()
    for copy in noisy_copies:
        copy.wait_recv()
    for row in range(PR):
        xn[row + 1, 1 : PC + 1] = dot(swap, raw_n[:, :, row].reshape(256, CH)).astype(BF).reshape(PC, NF, CH)
    n_halo = halo_copies(xn, 0)
    for copy in n_halo:
        copy.start()
    loads[0].wait()
    halo_end(xn, n_halo)
    for row in range(0, PR, 2):
        acc[row * 256 : row * 256 + 512] = conv(xn, v_in_n, row, 2)

    for copy in pick_copies:
        copy.wait_recv()
    pick_rows = pk[0]
    for q in range(1, 8):
        pick_rows = pick_rows + pk[q]
    pick_rows = jnp.broadcast_to(pick_rows[None], (16, NF, CH)).reshape(256, CH)
    pick_rows = jnp.concatenate([pick_rows, pick_rows], axis=1)
    choose = jnp.where((r_hi == c_lo) & (pick_rows == c_hi.astype(F32)), 1.0, 0.0).astype(BF)

    @pl.when(s == 0)
    def _():
        raw_c[...] = jnp.zeros(raw_c.shape, BF)

    @pl.when(s > 0)
    def _():
        for copy in clip_copies:
            copy.wait_recv()

    for row in range(PR):
        xc[row + 1, 1 : PC + 1] = dot(choose, raw_c[:, :, row].reshape(256, CH)).astype(BF).reshape(PC, NF, CH)
    c_halo = halo_copies(xc, 1)
    for copy in c_halo:
        copy.start()
    for load in loads[1:]:
        load.wait()
    halo_end(xc, c_halo)
    for row in range(0, PR, 2):
        v = acc[row * 256 : row * 256 + 512] + conv(xc, v_in_c, row, 2)
        hb[row + 1 : row + 3, 1 : PC + 1] = silu(v).astype(BF).reshape(2, PC, NF, CH)
    h_halo = halo_copies(hb, 2)
    for copy in h_halo:
        copy.start()
    halo_end(hb, h_halo)

    lane_r = lax.broadcasted_iota(jnp.int32, (CH, CH), 0)
    lane_c = lax.broadcasted_iota(jnp.int32, (CH, CH), 1)
    ones = jnp.full((CH, CH), 1.0, BF)
    by_head = jnp.where(lane_r // 64 == lane_c // 64, 1.0, 0.0).astype(BF)
    first_head = lane_c < 64
    same_pixel = lane_r // 16 == lane_c // 16
    same_pixel = jnp.concatenate([same_pixel, same_pixel], axis=0)
    scale = jnp.concatenate(
        [jnp.full((CH, CH), factors[0, 0] * (1 / 64)), jnp.full((CH, CH), factors[0, 1] * (1 / 64))], axis=0
    )
    for row in range(0, PR, 2):
        skip = hb[row + 1 : row + 3, 1 : PC + 1].reshape(512, CH).astype(F32)
        res[row * 256 : row * 256 + 512] = skip + conv(hb, v_mid, row, 2)

    def per_row(row, carry):
        at = pl.multiple_of(row * 256, 256)
        a = res[pl.ds(at, 256)]
        u = (a * lax.rsqrt(lane_sums(a * a, ones) * (1 / 128) + 1e-6)).astype(BF)
        qkv = dot(u, v_qkv[...])
        q, k, v = qkv[:, 0:CH], qkv[:, CH : 2 * CH], qkv[:, 2 * CH : 3 * CH].astype(BF)
        qn = (q * lax.rsqrt(lane_sums(q * q, by_head) * (1 / 64) + 1e-6)).astype(BF)
        kn = (k * lax.rsqrt(lane_sums(k * k, by_head) * (1 / 64) + 1e-6)).astype(BF)
        parts = []
        for g in range(2):
            qg, kg, vg = (z[g * CH : (g + 1) * CH] for z in (qn, kn, v))
            zero = jnp.zeros((CH, CH), BF)
            both = jnp.concatenate([jnp.where(first_head, qg, zero), jnp.where(first_head, zero, qg)], axis=0)
            sc = lax.dot_general(both, kg, (((1,), (1,)), ((), ())), preferred_element_type=F32) * scale
            sc = jnp.where(same_pixel, sc, -1e30)
            e = jnp.exp(sc - jnp.max(sc, axis=1, keepdims=True))
            total = jnp.sum(e, axis=1, keepdims=True)
            o = dot(e.astype(BF), vg) / total
            parts.append(jnp.where(first_head, o[:CH], o[CH:]).astype(BF))
        b = a + dot(jnp.concatenate(parts, axis=0), v_o[...])
        r = (b * lax.rsqrt(lane_sums(b * b, ones) * (1 / 128) + 1e-6)).astype(BF)
        m = silu(dot(r, v_up[...])).astype(BF)
        c = (b + dot(m, v_dn[...])).astype(BF)
        cb[row + 1, 1 : PC + 1] = c.reshape(PC, NF, CH)
        return carry

    lax.fori_loop(0, PR, per_row, 0)
    last_halo = halo_copies(cb, 3)
    for copy in last_halo:
        copy.start()
    halo_end(cb, last_halo)
    eps = [conv(cb, v_out, row, 2) for row in (0, 2)]
    for row in range(PR):
        part = eps[row // 2][(row % 2) * 256 : (row % 2) * 256 + 256].astype(BF)
        send_e[:, row] = dot(swap, part).astype(BF).reshape(NF, PC, CH)
    mine = eo.at[:, pl.ds(PR * i, PR), pl.ds(pl.multiple_of(PC * j, PC), PC), :]
    own_eps = pltpu.make_async_copy(send_e.at[pl.ds(2 * d, 2)], mine, s_e.at[0])
    eps_copies = []
    for k in range(1, 8):
        eps_copies.append(
            pltpu.make_async_remote_copy(
                src_ref=send_e.at[pl.ds(2 * in_group(k), 2)],
                dst_ref=mine,
                send_sem=s_e.at[k],
                recv_sem=r_e.at[k],
                device_id={"frame": in_group(k)},
                device_id_type=MESH,
            )
        )
        eps_copies[-1].start()
    own_eps.start()
    own_eps.wait()
    for copy in eps_copies:
        copy.wait_recv()
    out_eps = pltpu.make_async_copy(eo, eps_out.at[0], s_fin.at[0])
    out_eps.start()
    dv[...] = (coefs[0, 0] * xv[...].astype(F32) - coefs[0, 1] * eo[...].astype(F32)).astype(BF)
    out_den = pltpu.make_async_copy(dv, den_out.at[0], s_fin.at[1])
    out_den.start()
    for copy in pick_copies + noisy_copies + n_halo + c_halo + h_halo + last_halo + eps_copies:
        copy.wait_send()

    @pl.when(s < 3)
    def _():
        for copy in clip_copies:
            copy.wait_send()

    out_eps.wait()
    out_den.wait()


def local(x, clip, picks, w_in, w_mid, proj, factors, w_up, w_dn, w_out, coefs):
    hbm = pl.BlockSpec(memory_space=pl.ANY)
    smem = pl.BlockSpec(memory_space=pltpu.SMEM)
    patch = pltpu.VMEM((8, 2, PR, PC, CH), BF)
    padded = pltpu.VMEM((PR + 2, PC + 2, NF, CH), BF)
    clip_shape = x.shape[1:]
    dma = pltpu.SemaphoreType.DMA
    outs = jax.ShapeDtypeStruct(x.shape, BF)
    return pl.pallas_call(
        kernel,
        out_shape=(outs, outs),
        in_specs=[hbm, hbm, smem, hbm, hbm, hbm, smem, hbm, hbm, hbm, smem],
        out_specs=(hbm, hbm),
        scratch_shapes=[
            patch, patch, padded, padded, padded, padded,
            pltpu.VMEM((1024, CH), F32),
            pltpu.VMEM((1024, CH), F32),
            pltpu.VMEM((8, NF, CH), F32),
            pltpu.VMEM((NF, PR, PC, CH), BF),
            pltpu.VMEM(clip_shape, BF),
            pltpu.VMEM(clip_shape, BF),
            pltpu.VMEM(clip_shape, BF),
            pltpu.VMEM((3, 3, CH, CH), BF),
            pltpu.VMEM((3, 3, CH, CH), BF),
            pltpu.VMEM((3, 3, CH, CH), BF),
            pltpu.VMEM((CH, 3 * CH), BF),
            pltpu.VMEM((CH, CH), BF),
            pltpu.VMEM((CH, 4 * CH), BF),
            pltpu.VMEM((4 * CH, CH), BF),
            pltpu.VMEM((3, 3, CH, CH), BF),
            dma((11,)), dma((8,)), dma((8,)), dma((8,)), dma((8,)), dma((8,)), dma((8,)),
            dma((4, 8)), dma((4, 8)), dma((8,)), dma((8,)), dma((2,)),
        ],
        compiler_params=pltpu.CompilerParams(
            collective_id=0, has_side_effects=True, vmem_limit_bytes=40 * 1024 * 1024
        ),
        cost_estimate=pl.CostEstimate(flops=1_700_000_000, bytes_accessed=3_000_000, transcendentals=1_500_000),
        name="denoise",
    )(x, clip, picks, w_in, w_mid, proj, factors, w_up, w_dn, w_out, coefs)


def solution(mesh):
    clip = P("segment", "frame", "tile", None, None)
    kernel_spec = P("segment", None, None, None, None)
    in_specs = (
        clip, clip, P("segment", "frame"), kernel_spec, kernel_spec, P("segment", None, None, None),
        P("segment", None), P("segment", None, None), P("segment", None, None), kernel_spec, P("segment", None),
    )
    return jax.shard_map(local, mesh=mesh, in_specs=in_specs, out_specs=(clip, clip), check_vma=False)
```

```python
import functools

import jax
import jax.numpy as jnp
from jax import lax
from jax.experimental import pallas as pl
from jax.experimental.pallas import tpu as pltpu
from jax.sharding import PartitionSpec as P

MESH = pl.DeviceIdType.MESH
BF = jnp.bfloat16
F32 = jnp.float32
PR, PC, NF, CH = 4, 16, 16, 128
DIRS = [(-1, 0), (1, 0), (0, -1), (0, 1), (-1, -1), (-1, 1), (1, -1), (1, 1)]
ROWS, COLS, CORNERS = (0, 1), (2, 3), (4, 5, 6, 7)


def dot(a, b):
    return jnp.dot(a, b, preferred_element_type=F32)


def lane_sums(v, ones):
    hi = v.astype(BF)
    lo = (v - hi.astype(F32)).astype(BF)
    return dot(jnp.concatenate([hi, lo], axis=1), jnp.concatenate([ones, ones], axis=0))


def silu(v):
    half = 0.5 * v
    return half + half * jnp.tanh(half)


def kernel(
    x_hbm, clip_hbm, picks_hbm, w_in, w_mid, proj, factors_hbm, w_up, w_dn, w_out,
    eps_out,
    picks, factors, raw_n, raw_c, xn, xc, hb, cb, top, bot, lef, rig, acc, res, pk, send_e,
    v_in_n, v_in_c, v_mid, v_qkv, v_o, v_up, v_dn, v_out,
    s_w, s_pk, r_pk, s_c, r_c, s_n, r_n, s_h, r_h, s_e, r_e,
):
    s = lax.axis_index("segment")
    t = lax.axis_index("tile")
    d = lax.axis_index("frame")
    i, j = lax.rem(d, 2), lax.div(d, 2)
    big_row = 2 * t + i
    last_row = 2 * lax.axis_size("tile") - 1
    last_segment = lax.axis_size("segment") - 1

    def exists(dr, dc):
        row, col = big_row + dr, j + dc
        return (row >= 0) & (row <= last_row) & (col >= 0) & (col <= 3)

    def neighbour(dr, dc):
        row, col = big_row + dr, j + dc
        return {"tile": lax.div(row, 2), "frame": 2 * col + lax.rem(row, 2)}

    def in_group(k):
        return lax.rem(d + k, 8)

    def signal(device):
        pl.semaphore_signal(barrier, inc=1, device_id=device, device_id_type=MESH)

    for ref in (top, bot, lef, rig):
        ref[...] = jnp.zeros(ref.shape, BF)

    barrier = pltpu.get_barrier_semaphore()

    @pl.when(s > 0)
    def _():
        for k in range(8):
            signal({"segment": s - 1, "frame": in_group(k)})

    for k in range(1, 8):
        signal({"frame": in_group(k)})
    over = 2 * i - 1
    for dc in (-1, 0, 1):

        @pl.when(exists(over, dc))
        def _(dc=dc):
            signal(neighbour(over, dc))

    weights = [
        (picks_hbm, picks),
        (w_in.at[0, :, :, 0:CH, :], v_in_n),
        (w_in.at[0, :, :, CH : 2 * CH, :], v_in_c),
        (factors_hbm, factors),
        (w_mid.at[0], v_mid),
        (proj.at[0, 0], v_qkv.at[:, 0:CH]),
        (proj.at[0, 1], v_qkv.at[:, CH : 2 * CH]),
        (proj.at[0, 2], v_qkv.at[:, 2 * CH : 3 * CH]),
        (proj.at[0, 3], v_o),
        (w_up.at[0], v_up),
        (w_dn.at[0], v_dn),
        (w_out.at[0], v_out),
    ]
    loads = [pltpu.make_async_copy(a, b, s_w.at[q]) for q, (a, b) in enumerate(weights)]
    for load in loads:
        load.start()
    for buf in (xn, xc, hb, cb):
        buf[0] = jnp.zeros((PC + 2, NF, CH), BF)
        buf[PR + 1] = jnp.zeros((PC + 2, NF, CH), BF)
        buf[:, 0:1] = jnp.zeros((PR + 2, 1, NF, CH), BF)
        buf[:, PC + 1 : PC + 2] = jnp.zeros((PR + 2, 1, NF, CH), BF)
    partners = 7 + jnp.where(s < last_segment, 8, 0)
    for dc in (-1, 0, 1):
        partners = partners + jnp.where(exists(over, dc), 1, 0)
    pl.semaphore_wait(barrier, partners)

    def patch_of(ref, c):
        return ref.at[0, :, pl.ds(PR * lax.rem(c, 2), PR), pl.ds(pl.multiple_of(PC * lax.div(c, 2), PC), PC), :]

    def clip_copy(k):
        return pltpu.make_async_remote_copy(
            src_ref=patch_of(clip_hbm, in_group(k)),
            dst_ref=raw_c.at[d],
            send_sem=s_c.at[k],
            recv_sem=r_c.at[k],
            device_id={"segment": s + 1, "frame": in_group(k)},
            device_id_type=MESH,
        )

    @pl.when(s < last_segment)
    def _():
        for k in range(8):
            clip_copy(k).start()

    pick_copies, noisy_copies = [], []
    own_noisy = pltpu.make_async_copy(patch_of(x_hbm, d), raw_n.at[d], s_n.at[0])
    own_noisy.start()
    for k in range(1, 8):
        noisy_copies.append(
            pltpu.make_async_remote_copy(
                src_ref=patch_of(x_hbm, in_group(k)),
                dst_ref=raw_n.at[d],
                send_sem=s_n.at[k],
                recv_sem=r_n.at[k],
                device_id={"frame": in_group(k)},
                device_id_type=MESH,
            )
        )
        noisy_copies[-1].start()
    loads[0].wait()
    frame_row = lax.broadcasted_iota(jnp.int32, (NF, CH), 0)
    pk[d] = jnp.where(frame_row == 2 * d, picks[0, 0], jnp.where(frame_row == 2 * d + 1, picks[0, 1], 0)).astype(F32)
    for k in range(1, 8):
        pick_copies.append(
            pltpu.make_async_remote_copy(
                src_ref=pk.at[d],
                dst_ref=pk.at[d],
                send_sem=s_pk.at[k],
                recv_sem=r_pk.at[k],
                device_id={"frame": in_group(k)},
                device_id_type=MESH,
            )
        )
        pick_copies[-1].start()

    r_i = lax.broadcasted_iota(jnp.int32, (256, 256), 0)
    c_i = lax.broadcasted_iota(jnp.int32, (256, 256), 1)
    r_hi, r_lo, c_hi, c_lo = r_i // 16, r_i % 16, c_i // 16, c_i % 16
    swap = jnp.where((r_hi == c_lo) & (r_lo == c_hi), 1.0, 0.0).astype(BF)

    def halo_copy(buf, n, k):
        inner = slice(1, PC + 1)
        rows = slice(1, PR + 1)
        ends = [
            (buf.at[1, inner], bot.at[n, inner]),
            (buf.at[PR, inner], top.at[n, inner]),
            (buf.at[rows, 1], rig.at[n, rows]),
            (buf.at[rows, PC], lef.at[n, rows]),
            (buf.at[1, 1], bot.at[n, PC + 1]),
            (buf.at[1, PC], bot.at[n, 0]),
            (buf.at[PR, 1], top.at[n, PC + 1]),
            (buf.at[PR, PC], top.at[n, 0]),
        ]
        src, dst = ends[k]
        return pltpu.make_async_remote_copy(
            src_ref=src,
            dst_ref=dst,
            send_sem=s_h.at[n, k],
            recv_sem=r_h.at[n, k],
            device_id=neighbour(*DIRS[k]),
            device_id_type=MESH,
        )

    def halo_start(buf, n):
        for k in range(8):
            pl.when(exists(*DIRS[k]))(halo_copy(buf, n, k).start)

    def halo_wait(buf, n, which):
        for k in which:
            dr, dc = DIRS[k]
            pl.when(exists(-dr, -dc))(halo_copy(buf, n, k).wait_recv)

    def halo_sent(buf, n):
        for k in range(8):
            pl.when(exists(*DIRS[k]))(halo_copy(buf, n, k).wait_send)

    def conv(buf, w, row, rows):
        n = rows * PC * NF
        parts = [
            buf[row + dr : row + dr + rows, dc : dc + PC].reshape(n, CH) for dr in range(3) for dc in range(3)
        ]
        return dot(jnp.concatenate(parts, axis=1), w[...].reshape(9 * CH, CH)).reshape(rows, PC, NF, CH)

    def add_rows(to, n, w):
        for row, ref, tap in ((0, top, 0), (PR - 1, bot, 2)):
            parts = [ref[n, dc : dc + PC].reshape(PC * NF, CH) for dc in range(3)]
            to[row] += dot(jnp.concatenate(parts, axis=1), w[tap].reshape(3 * CH, CH)).reshape(PC, NF, CH)

    def add_cols(to, n, w):
        for col, ref, tap in ((0, lef, 0), (PC - 1, rig, 2)):
            parts = [ref[n, dr : dr + PR].reshape(PR * NF, CH) for dr in range(3)]
            to[:, col] += dot(jnp.concatenate(parts, axis=1), w[:, tap].reshape(3 * CH, CH)).reshape(PR, NF, CH)

    own_noisy.wait()
    for copy in noisy_copies:
        copy.wait_recv()
    for row in range(PR):
        xn[row + 1, 1 : PC + 1] = dot(swap, raw_n[:, :, row].reshape(256, CH)).astype(BF).reshape(PC, NF, CH)
    halo_start(xn, 0)
    loads[1].wait()
    for row in (0, 2):
        acc[row : row + 2] = conv(xn, v_in_n, row, 2)

    for copy in pick_copies:
        copy.wait_recv()
    pick_rows = pk[0]
    for q in range(1, 8):
        pick_rows = pick_rows + pk[q]
    pick_rows = jnp.broadcast_to(pick_rows[None], (16, NF, CH)).reshape(256, CH)
    pick_rows = jnp.concatenate([pick_rows, pick_rows], axis=1)
    choose = jnp.where((r_hi == c_lo) & (pick_rows == c_hi.astype(F32)), 1.0, 0.0).astype(BF)

    @pl.when(s == 0)
    def _():
        raw_c[...] = jnp.zeros(raw_c.shape, BF)

    @pl.when(s > 0)
    def _():
        for k in range(8):
            clip_copy(k).wait_recv()

    for row in range(PR):
        xc[row + 1, 1 : PC + 1] = dot(choose, raw_c[:, :, row].reshape(256, CH)).astype(BF).reshape(PC, NF, CH)
    halo_start(xc, 1)
    for load in loads[2:]:
        load.wait()
    for row in (0, 2):
        acc[row : row + 2] += conv(xc, v_in_c, row, 2)
    halo_wait(xn, 0, range(8))
    add_rows(acc, 0, v_in_n)
    add_cols(acc, 0, v_in_n)
    halo_wait(xc, 1, range(8))
    add_rows(acc, 1, v_in_c)
    add_cols(acc, 1, v_in_c)
    hb[1 : PR + 1, 1 : PC + 1] = silu(acc[...]).astype(BF)
    halo_start(hb, 2)

    lane_r = lax.broadcasted_iota(jnp.int32, (CH, CH), 0)
    lane_c = lax.broadcasted_iota(jnp.int32, (CH, CH), 1)
    ones = jnp.full((CH, CH), 1.0, BF)
    by_head = jnp.where(lane_r // 64 == lane_c // 64, 1.0, 0.0).astype(BF)
    first_head = lane_c < 64
    other_pixel = jnp.where(lane_r // 16 == lane_c // 16, 0.0, -1e30)
    for row in (0, 2):
        skip = hb[row + 1 : row + 3, 1 : PC + 1].astype(F32)
        res[row : row + 2] = skip + conv(hb, v_mid, row, 2)
    halo_sent(xn, 0)
    halo_sent(xc, 1)

    def two_rows(rows):
        a = jnp.concatenate([res[row].reshape(256, CH) for row in rows], axis=0)
        u = (a * lax.rsqrt(lane_sums(a * a, ones) * (1 / 128) + 1e-6)).astype(BF)
        qkv = dot(u, v_qkv[...])
        q, k, v = qkv[:, 0:CH], qkv[:, CH : 2 * CH], qkv[:, 2 * CH : 3 * CH].astype(BF)
        qn = (q * lax.rsqrt(lane_sums(q * q, by_head) * (1 / 64) + 1e-6)).astype(BF)
        kn = (k * lax.rsqrt(lane_sums(k * k, by_head) * (1 / 64) + 1e-6)).astype(BF)
        parts = []
        zero = jnp.zeros((CH, CH), BF)
        for g in range(4):
            qg, kg, vg = (z[g * CH : (g + 1) * CH] for z in (qn, kn, v))
            both = jnp.concatenate([jnp.where(first_head, qg, zero), jnp.where(first_head, zero, qg)], axis=0)
            sc = lax.dot_general(both, kg, (((1,), (1,)), ((), ())), preferred_element_type=F32)
            sc = jnp.concatenate(
                [sc[h * CH : (h + 1) * CH] * (factors[0, h] * (1 / 64)) + other_pixel for h in range(2)], axis=0
            )
            e = jnp.exp(sc - jnp.max(sc, axis=1, keepdims=True))
            total = jnp.sum(e, axis=1, keepdims=True)
            o = dot(e.astype(BF), vg) / total
            parts.append(jnp.where(first_head, o[:CH], o[CH:]).astype(BF))
        b = a + dot(jnp.concatenate(parts, axis=0), v_o[...])
        r = (b * lax.rsqrt(lane_sums(b * b, ones) * (1 / 128) + 1e-6)).astype(BF)
        m = silu(dot(r, v_up[...])).astype(BF)
        c = (b + dot(m, v_dn[...])).astype(BF)
        for q, row in enumerate(rows):
            cb[row + 1, 1 : PC + 1] = c[q * 256 : (q + 1) * 256].reshape(PC, NF, CH)

    halo_wait(hb, 2, COLS)
    add_cols(res, 2, v_mid)
    two_rows((1, 2))
    halo_wait(hb, 2, ROWS + CORNERS)
    add_rows(res, 2, v_mid)
    two_rows((0, 3))
    halo_start(cb, 3)
    halo_sent(hb, 2)
    for row in (0, 2):
        acc[row : row + 2] = conv(cb, v_out, row, 2)
    halo_wait(cb, 3, COLS)
    add_cols(acc, 3, v_out)

    def eps_copy(k, n, rows):
        size = rows.stop - rows.start
        src = send_e.at[pl.ds(2 * in_group(k), 2), rows]
        dst = eps_out.at[0, :, pl.ds(PR * i + rows.start, size), pl.ds(pl.multiple_of(PC * j, PC), PC), :]
        if k == 0:
            return pltpu.make_async_copy(src, dst, s_e.at[n, 0])
        return pltpu.make_async_remote_copy(
            src_ref=src,
            dst_ref=dst,
            send_sem=s_e.at[n, k],
            recv_sem=r_e.at[n, k],
            device_id={"frame": in_group(k)},
            device_id_type=MESH,
        )

    eps_copies = []

    def give_back(n, rows):
        for row in range(rows.start, rows.stop):
            part = dot(swap, acc[row].reshape(256, CH).astype(BF)).astype(BF)
            send_e[:, row] = part.reshape(NF, PC, CH)
        for k in (*range(1, 8), 0):
            eps_copies.append((k, eps_copy(k, n, rows)))
            eps_copies[-1][1].start()

    give_back(0, slice(1, 3))
    halo_wait(cb, 3, ROWS + CORNERS)
    add_rows(acc, 3, v_out)
    give_back(1, slice(0, 1))
    give_back(2, slice(3, 4))
    for copy in pick_copies + noisy_copies:
        copy.wait_send()

    @pl.when(s < last_segment)
    def _():
        for k in range(8):
            clip_copy(k).wait_send()

    halo_sent(cb, 3)
    for k, copy in eps_copies:
        copy.wait()


def local(x, clip, picks, w_in, w_mid, proj, factors, w_up, w_dn, w_out, coefs):
    hbm = pl.BlockSpec(memory_space=pltpu.HBM)
    patch = pltpu.VMEM((8, 2, PR, PC, CH), BF)
    padded = pltpu.VMEM((PR + 2, PC + 2, NF, CH), BF)
    side = pltpu.VMEM((4, PC + 2, NF, CH), BF)
    upright = pltpu.VMEM((4, PR + 2, NF, CH), BF)
    sums = pltpu.VMEM((PR, PC, NF, CH), F32)
    taps = pltpu.VMEM((3, 3, CH, CH), BF)
    dma = pltpu.SemaphoreType.DMA
    eps = pl.pallas_call(
        kernel,
        out_shape=jax.ShapeDtypeStruct(x.shape, BF),
        in_specs=[hbm] * 10,
        out_specs=hbm,
        scratch_shapes=[
            pltpu.SMEM((1, 2), jnp.int32),
            pltpu.SMEM((1, 2), F32),
            patch, patch, padded, padded, padded, padded, side, side, upright, upright, sums, sums,
            pltpu.VMEM((8, NF, CH), F32),
            pltpu.VMEM((NF, PR, PC, CH), BF),
            taps, taps, taps,
            pltpu.VMEM((CH, 3 * CH), BF),
            pltpu.VMEM((CH, CH), BF),
            pltpu.VMEM((CH, 4 * CH), BF),
            pltpu.VMEM((4 * CH, CH), BF),
            taps,
            dma((12,)), dma((8,)), dma((8,)), dma((8,)), dma((8,)), dma((8,)), dma((8,)),
            dma((4, 8)), dma((4, 8)), dma((3, 8)), dma((3, 8)),
        ],
        compiler_params=pltpu.CompilerParams(
            collective_id=0, has_side_effects=True, vmem_limit_bytes=60 * 1024 * 1024
        ),
        cost_estimate=pl.CostEstimate(flops=1_700_000_000, bytes_accessed=3_000_000, transcendentals=1_500_000),
        name="denoise",
    )(x, clip, picks, w_in, w_mid, proj, factors, w_up, w_dn, w_out)
    denoised = coefs[0, 0] * x.astype(F32) - coefs[0, 1] * eps.astype(F32)
    return denoised.astype(BF), eps


def solution(mesh):
    clip = P("segment", "frame", "tile", None, None)
    kernel_spec = P("segment", None, None, None, None)
    in_specs = (
        clip, clip, P("segment", "frame"), kernel_spec, kernel_spec, P("segment", None, None, None),
        P("segment", None), P("segment", None, None), P("segment", None, None), kernel_spec, P("segment", None),
    )
    return jax.shard_map(local, mesh=mesh, in_specs=in_specs, out_specs=(clip, clip), check_vma=False)
```

```python
import functools

import jax
import jax.numpy as jnp
from jax import lax
from jax.experimental import pallas as pl
from jax.experimental.pallas import tpu as pltpu
from jax.sharding import PartitionSpec as P

MESH = pl.DeviceIdType.MESH
BF = jnp.bfloat16
F32 = jnp.float32
PR, PC, NF, CH = 4, 16, 16, 128
TR, W = 8, 64
DIRS = [(-1, 0), (1, 0), (0, -1), (0, 1), (-1, -1), (-1, 1), (1, -1), (1, 1)]
ROWS, COLS, CORNERS = (0, 1), (2, 3), (4, 5, 6, 7)


def dot(a, b):
    return jnp.dot(a, b, preferred_element_type=F32)


def lane_sums(v, ones):
    hi = v.astype(BF)
    lo = (v - hi.astype(F32)).astype(BF)
    return dot(jnp.concatenate([hi, lo], axis=1), jnp.concatenate([ones, ones], axis=0))


def silu(v):
    half = 0.5 * v
    return half + half * jnp.tanh(half)


def kernel(
    x_hbm, clip_hbm, picks_hbm, w_in, w_mid, proj, factors_hbm, w_up, w_dn, w_out, coefs_hbm,
    den_out, eps_out,
    picks, factors, coefs, raw_n, raw_c, xn, xc, hb, top, bot, lef, rig, acc, res, pk, send_c, frames_c, xv,
    v_in_n, v_in_c, v_mid, v_qkv, v_o, v_up, v_dn, v_out,
    s_w, s_pk, r_pk, s_c, r_c, s_n, r_n, s_h, r_h, s_e, r_e, s_o, r_o,
):
    s = lax.axis_index("segment")
    t = lax.axis_index("tile")
    d = lax.axis_index("frame")
    i, j = lax.rem(d, 2), lax.div(d, 2)
    big_row = 2 * t + i
    last_tile = lax.axis_size("tile") - 1
    last_row = 2 * last_tile + 1
    last_segment = lax.axis_size("segment") - 1

    def exists(dr, dc):
        row, col = big_row + dr, j + dc
        return (row >= 0) & (row <= last_row) & (col >= 0) & (col <= 3)

    def neighbour(dr, dc):
        row, col = big_row + dr, j + dc
        return {"tile": lax.div(row, 2), "frame": 2 * col + lax.rem(row, 2)}

    def in_group(k):
        return lax.rem(d + k, 8)

    def signal(device):
        pl.semaphore_signal(barrier, inc=1, device_id=device, device_id_type=MESH)

    for ref in (top, bot, lef, rig):
        ref[...] = jnp.zeros(ref.shape, BF)
    frames_c[:, 0:1] = jnp.zeros((2, 1, W, CH), BF)
    frames_c[:, TR + 1 :] = jnp.zeros((2, 1, W, CH), BF)

    barrier = pltpu.get_barrier_semaphore()

    @pl.when(s > 0)
    def _():
        for k in range(8):
            signal({"segment": s - 1, "frame": in_group(k)})

    for k in range(1, 8):
        signal({"frame": in_group(k)})

    @pl.when(t > 0)
    def _():
        for q in range(4):
            signal({"tile": t - 1, "frame": 2 * q + 1})

    @pl.when(t < last_tile)
    def _():
        for q in range(4):
            signal({"tile": t + 1, "frame": 2 * q})

    over = t + 2 * i - 1
    over_exists = (over >= 0) & (over <= last_tile)

    weights = [
        (picks_hbm, picks),
        (w_in.at[0, :, :, 0:CH, :], v_in_n),
        (w_in.at[0, :, :, CH : 2 * CH, :], v_in_c),
        (factors_hbm, factors),
        (w_mid.at[0], v_mid),
        (proj.at[0, 0], v_qkv.at[:, 0:CH]),
        (proj.at[0, 1], v_qkv.at[:, CH : 2 * CH]),
        (proj.at[0, 2], v_qkv.at[:, 2 * CH : 3 * CH]),
        (proj.at[0, 3], v_o),
        (w_up.at[0], v_up),
        (w_dn.at[0], v_dn),
        *((w_out.at[0, :, q], v_out.at[:, :, q * CH : (q + 1) * CH]) for q in range(3)),
        (coefs_hbm, coefs),
        (x_hbm.at[0], xv),
    ]
    loads = [pltpu.make_async_copy(a, b, s_w.at[q]) for q, (a, b) in enumerate(weights)]
    for load in loads:
        load.start()
    for buf in (xn, xc, hb):
        buf[0] = jnp.zeros((PC + 2, NF, CH), BF)
        buf[PR + 1] = jnp.zeros((PC + 2, NF, CH), BF)
        buf[:, 0:1] = jnp.zeros((PR + 2, 1, NF, CH), BF)
        buf[:, PC + 1 : PC + 2] = jnp.zeros((PR + 2, 1, NF, CH), BF)
    pl.semaphore_wait(barrier, 7 + jnp.where(s < last_segment, 8, 0) + jnp.where(over_exists, 8, 0))

    def patch_of(ref, c):
        return ref.at[0, :, pl.ds(PR * lax.rem(c, 2), PR), pl.ds(pl.multiple_of(PC * lax.div(c, 2), PC), PC), :]

    def clip_copy(k):
        return pltpu.make_async_remote_copy(
            src_ref=patch_of(clip_hbm, in_group(k)),
            dst_ref=raw_c.at[d],
            send_sem=s_c.at[k],
            recv_sem=r_c.at[k],
            device_id={"segment": s + 1, "frame": in_group(k)},
            device_id_type=MESH,
        )

    @pl.when(s < last_segment)
    def _():
        for k in range(8):
            clip_copy(k).start()

    pick_copies, noisy_copies = [], []
    own_noisy = pltpu.make_async_copy(patch_of(x_hbm, d), raw_n.at[d], s_n.at[0])
    own_noisy.start()
    for k in range(1, 8):
        noisy_copies.append(
            pltpu.make_async_remote_copy(
                src_ref=patch_of(x_hbm, in_group(k)),
                dst_ref=raw_n.at[d],
                send_sem=s_n.at[k],
                recv_sem=r_n.at[k],
                device_id={"frame": in_group(k)},
                device_id_type=MESH,
            )
        )
        noisy_copies[-1].start()
    loads[0].wait()
    frame_row = lax.broadcasted_iota(jnp.int32, (NF, CH), 0)
    pk[d] = jnp.where(frame_row == 2 * d, picks[0, 0], jnp.where(frame_row == 2 * d + 1, picks[0, 1], 0)).astype(F32)
    for k in range(1, 8):
        pick_copies.append(
            pltpu.make_async_remote_copy(
                src_ref=pk.at[d],
                dst_ref=pk.at[d],
                send_sem=s_pk.at[k],
                recv_sem=r_pk.at[k],
                device_id={"frame": in_group(k)},
                device_id_type=MESH,
            )
        )
        pick_copies[-1].start()

    r_i = lax.broadcasted_iota(jnp.int32, (256, 256), 0)
    c_i = lax.broadcasted_iota(jnp.int32, (256, 256), 1)
    r_hi, r_lo, c_hi, c_lo = r_i // 16, r_i % 16, c_i // 16, c_i % 16
    swap = jnp.where((r_hi == c_lo) & (r_lo == c_hi), 1.0, 0.0).astype(BF)

    def halo_copy(buf, n, k):
        inner = slice(1, PC + 1)
        rows = slice(1, PR + 1)
        ends = [
            (buf.at[1, inner], bot.at[n, inner]),
            (buf.at[PR, inner], top.at[n, inner]),
            (buf.at[rows, 1], rig.at[n, rows]),
            (buf.at[rows, PC], lef.at[n, rows]),
            (buf.at[1, 1], bot.at[n, PC + 1]),
            (buf.at[1, PC], bot.at[n, 0]),
            (buf.at[PR, 1], top.at[n, PC + 1]),
            (buf.at[PR, PC], top.at[n, 0]),
        ]
        src, dst = ends[k]
        return pltpu.make_async_remote_copy(
            src_ref=src,
            dst_ref=dst,
            send_sem=s_h.at[n, k],
            recv_sem=r_h.at[n, k],
            device_id=neighbour(*DIRS[k]),
            device_id_type=MESH,
        )

    def halo_start(buf, n):
        for k in COLS + CORNERS + ROWS:
            pl.when(exists(*DIRS[k]))(halo_copy(buf, n, k).start)

    def halo_wait(buf, n, which):
        for k in which:
            dr, dc = DIRS[k]
            pl.when(exists(-dr, -dc))(halo_copy(buf, n, k).wait_recv)

    def halo_sent(buf, n):
        for k in range(8):
            pl.when(exists(*DIRS[k]))(halo_copy(buf, n, k).wait_send)

    def conv(buf, w, row, rows):
        n = rows * PC * NF
        parts = [
            buf[row + dr : row + dr + rows, dc : dc + PC].reshape(n, CH) for dr in range(3) for dc in range(3)
        ]
        return dot(jnp.concatenate(parts, axis=1), w[...].reshape(9 * CH, CH)).reshape(rows, PC, NF, CH)

    def add_rows(to, n, w):
        for row, ref, tap in ((0, top, 0), (PR - 1, bot, 2)):
            parts = [ref[n, dc : dc + PC].reshape(PC * NF, CH) for dc in range(3)]
            to[row] += dot(jnp.concatenate(parts, axis=1), w[tap].reshape(3 * CH, CH)).reshape(PC, NF, CH)

    def add_cols(to, n, w):
        for col, ref, tap in ((0, lef, 0), (PC - 1, rig, 2)):
            parts = [ref[n, dr : dr + PR].reshape(PR * NF, CH) for dr in range(3)]
            to[:, col] += dot(jnp.concatenate(parts, axis=1), w[:, tap].reshape(3 * CH, CH)).reshape(PR, NF, CH)

    own_noisy.wait()
    for copy in noisy_copies:
        copy.wait_recv()
    for row in range(PR):
        xn[row + 1, 1 : PC + 1] = dot(swap, raw_n[:, :, row].reshape(256, CH)).astype(BF).reshape(PC, NF, CH)
    halo_start(xn, 0)
    loads[1].wait()
    for row in (0, 2):
        acc[row : row + 2] = conv(xn, v_in_n, row, 2)

    for copy in pick_copies:
        copy.wait_recv()
    pick_rows = pk[0]
    for q in range(1, 8):
        pick_rows = pick_rows + pk[q]
    pick_rows = jnp.broadcast_to(pick_rows[None], (16, NF, CH)).reshape(256, CH)
    pick_rows = jnp.concatenate([pick_rows, pick_rows], axis=1)
    choose = jnp.where((r_hi == c_lo) & (pick_rows == c_hi.astype(F32)), 1.0, 0.0).astype(BF)

    @pl.when(s == 0)
    def _():
        raw_c[...] = jnp.zeros(raw_c.shape, BF)

    @pl.when(s > 0)
    def _():
        for k in range(8):
            clip_copy(k).wait_recv()

    for row in range(PR):
        xc[row + 1, 1 : PC + 1] = dot(choose, raw_c[:, :, row].reshape(256, CH)).astype(BF).reshape(PC, NF, CH)
    halo_start(xc, 1)
    for load in loads[2:]:
        load.wait()
    for row in (0, 2):
        acc[row : row + 2] += conv(xc, v_in_c, row, 2)
    halo_wait(xn, 0, range(8))
    add_rows(acc, 0, v_in_n)
    add_cols(acc, 0, v_in_n)
    halo_wait(xc, 1, range(8))
    add_rows(acc, 1, v_in_c)
    add_cols(acc, 1, v_in_c)
    hb[1 : PR + 1, 1 : PC + 1] = silu(acc[...]).astype(BF)
    halo_start(hb, 2)

    lane_r = lax.broadcasted_iota(jnp.int32, (CH, CH), 0)
    lane_c = lax.broadcasted_iota(jnp.int32, (CH, CH), 1)
    ones = jnp.full((CH, CH), 1.0, BF)
    by_head = jnp.where(lane_r // 64 == lane_c // 64, 1.0, 0.0).astype(BF)
    first_head = lane_c < 64
    other_pixel = jnp.where(lane_r // 16 == lane_c // 16, 0.0, -1e30)
    for row in (0, 2):
        skip = hb[row + 1 : row + 3, 1 : PC + 1].astype(F32)
        res[row : row + 2] = skip + conv(hb, v_mid, row, 2)
    halo_sent(xn, 0)
    halo_sent(xc, 1)

    def two_rows(rows):
        a = jnp.concatenate([res[row].reshape(256, CH) for row in rows], axis=0)
        u = (a * lax.rsqrt(lane_sums(a * a, ones) * (1 / 128) + 1e-6)).astype(BF)
        qkv = dot(u, v_qkv[...])
        q, k, v = qkv[:, 0:CH], qkv[:, CH : 2 * CH], qkv[:, 2 * CH : 3 * CH].astype(BF)
        qn = (q * lax.rsqrt(lane_sums(q * q, by_head) * (1 / 64) + 1e-6)).astype(BF)
        kn = (k * lax.rsqrt(lane_sums(k * k, by_head) * (1 / 64) + 1e-6)).astype(BF)
        parts = []
        zero = jnp.zeros((CH, CH), BF)
        for g in range(4):
            qg, kg, vg = (z[g * CH : (g + 1) * CH] for z in (qn, kn, v))
            both = jnp.concatenate([jnp.where(first_head, qg, zero), jnp.where(first_head, zero, qg)], axis=0)
            sc = lax.dot_general(both, kg, (((1,), (1,)), ((), ())), preferred_element_type=F32)
            sc = jnp.concatenate(
                [sc[h * CH : (h + 1) * CH] * (factors[0, h] * (1 / 64)) + other_pixel for h in range(2)], axis=0
            )
            e = jnp.exp(sc - jnp.max(sc, axis=1, keepdims=True))
            total = jnp.sum(e, axis=1, keepdims=True)
            o = dot(e.astype(BF), vg) / total
            parts.append(jnp.where(first_head, o[:CH], o[CH:]).astype(BF))
        b = a + dot(jnp.concatenate(parts, axis=0), v_o[...])
        r = (b * lax.rsqrt(lane_sums(b * b, ones) * (1 / 128) + 1e-6)).astype(BF)
        m = silu(dot(r, v_up[...])).astype(BF)
        c = (b + dot(m, v_dn[...])).astype(BF)
        for q, row in enumerate(rows):
            part = dot(swap, c[q * 256 : (q + 1) * 256]).astype(BF)
            send_c[:, row] = part.reshape(NF, PC, CH)

    def back_copy(n, k, first, size, to_row, device):
        frame = device["frame"]
        src = send_c.at[pl.ds(2 * frame, 2), first : first + size]
        dst = frames_c.at[:, pl.ds(to_row, size), pl.ds(pl.multiple_of(PC * j, PC), PC), :]
        return pltpu.make_async_remote_copy(
            src_ref=src,
            dst_ref=dst,
            send_sem=s_e.at[n, k],
            recv_sem=r_e.at[n, k],
            device_id=device,
            device_id_type=MESH,
        )

    def give_back(n, first, size):
        copies = [back_copy(n, k, first, size, 1 + PR * i + first, {"frame": in_group(k)}) for k in range(1, 8)]
        for copy in copies:
            copy.start()
        own = pltpu.make_async_copy(
            send_c.at[pl.ds(2 * d, 2), first : first + size],
            frames_c.at[:, pl.ds(1 + PR * i + first, size), pl.ds(pl.multiple_of(PC * j, PC), PC), :],
            s_e.at[n, 0],
        )
        own.start()
        return [*copies, own]

    halo_wait(hb, 2, COLS)
    add_cols(res, 2, v_mid)
    two_rows((1, 2))
    back = give_back(0, 1, 2)
    halo_wait(hb, 2, ROWS + CORNERS)
    add_rows(res, 2, v_mid)
    two_rows((0, 3))

    def over_copy(k, upper):
        first, to_row = (0, TR + 1) if upper else (PR - 1, 0)
        device = {"tile": over, "frame": in_group(k)}
        src = send_c.at[pl.ds(2 * in_group(k), 2), first : first + 1]
        dst = frames_c.at[:, to_row : to_row + 1, pl.ds(pl.multiple_of(PC * j, PC), PC), :]
        return pltpu.make_async_remote_copy(
            src_ref=src,
            dst_ref=dst,
            send_sem=s_o.at[k],
            recv_sem=r_o.at[1 if upper else 0, j],
            device_id=device,
            device_id_type=MESH,
        )

    for upper in (True, False):

        @pl.when(over_exists & (i == (0 if upper else 1)))
        def _(upper=upper):
            for k in range(8):
                over_copy(k, upper).start()

    back += give_back(1, 0, 1)
    back += give_back(2, PR - 1, 1)
    halo_sent(hb, 2)
    for copy in pick_copies + noisy_copies:
        copy.wait_send()

    @pl.when(s < last_segment)
    def _():
        for k in range(8):
            clip_copy(k).wait_send()

    for copy in back:
        copy.wait()

    def over_arrived(side, q, to_row):
        at = frames_c.at[:, to_row : to_row + 1, q * PC : (q + 1) * PC, :]
        pltpu.make_async_remote_copy(
            src_ref=at, dst_ref=at, send_sem=s_o.at[0], recv_sem=r_o.at[side, q], device_id={"frame": d}, device_id_type=MESH
        ).wait_recv()

    @pl.when(t > 0)
    def _():
        for q in range(4):
            over_arrived(0, q, 0)

    @pl.when(t < last_tile)
    def _():
        for q in range(4):
            over_arrived(1, q, TR + 1)

    column = lax.rem(lax.broadcasted_iota(jnp.int32, (TR * W, CH), 0), W)
    for f in range(2):
        rows = [frames_c[f, dr : dr + TR].reshape(TR * W, CH) for dr in range(3)]
        out = dot(jnp.concatenate(rows, axis=1), v_out[...].reshape(3 * CH, 3 * CH))
        left = jnp.where(column == 0, 0.0, pltpu.roll(out[:, 0:CH], 1, 0))
        right = jnp.where(column == W - 1, 0.0, pltpu.roll(out[:, 2 * CH :], TR * W - 1, 0))
        eps = out[:, CH : 2 * CH] + left + right
        eps_out[0, f] = eps.astype(BF).reshape(TR, W, CH)
        noisy = xv[f].reshape(TR * W, CH).astype(F32)
        den_out[0, f] = (coefs[0, 0] * noisy - coefs[0, 1] * eps).astype(BF).reshape(TR, W, CH)

    for upper in (True, False):

        @pl.when(over_exists & (i == (0 if upper else 1)))
        def _(upper=upper):
            for k in range(8):
                over_copy(k, upper).wait_send()


def put_out(den, eps, den_out, eps_out, sems):
    copies = [pltpu.make_async_copy(a, b, sems.at[q]) for q, (a, b) in enumerate(((den, den_out), (eps, eps_out)))]
    for copy in copies:
        copy.start()
    for copy in copies:
        copy.wait()


def local(x, clip, picks, w_in, w_mid, proj, factors, w_up, w_dn, w_out, coefs):
    args = (x, clip, picks, w_in, w_mid, proj, factors, w_up, w_dn, w_out, coefs)
    args = [pltpu.with_memory_space_constraint(z, pltpu.HBM) for z in args]
    hbm = pl.BlockSpec(memory_space=pltpu.HBM)
    vmem = pl.BlockSpec(memory_space=pltpu.VMEM)
    patch = pltpu.VMEM((8, 2, PR, PC, CH), BF)
    padded = pltpu.VMEM((PR + 2, PC + 2, NF, CH), BF)
    side = pltpu.VMEM((3, PC + 2, NF, CH), BF)
    upright = pltpu.VMEM((3, PR + 2, NF, CH), BF)
    sums = pltpu.VMEM((PR, PC, NF, CH), F32)
    taps = pltpu.VMEM((3, 3, CH, CH), BF)
    dma = pltpu.SemaphoreType.DMA
    den, eps = pl.pallas_call(
        kernel,
        out_shape=(pltpu.VMEM(x.shape, BF), pltpu.VMEM(x.shape, BF)),
        in_specs=[hbm] * 11,
        out_specs=(vmem, vmem),
        scratch_shapes=[
            pltpu.SMEM((1, 2), jnp.int32),
            pltpu.SMEM((1, 2), F32),
            pltpu.SMEM((1, 2), F32),
            patch, patch, padded, padded, padded, side, side, upright, upright, sums, sums,
            pltpu.VMEM((8, NF, CH), F32),
            pltpu.VMEM((NF, PR, PC, CH), BF),
            pltpu.VMEM((2, TR + 2, W, CH), BF),
            pltpu.VMEM(x.shape[1:], BF),
            taps, taps, taps,
            pltpu.VMEM((CH, 3 * CH), BF),
            pltpu.VMEM((CH, CH), BF),
            pltpu.VMEM((CH, 4 * CH), BF),
            pltpu.VMEM((4 * CH, CH), BF),
            pltpu.VMEM((3, CH, 3 * CH), BF),
            dma((16,)), dma((8,)), dma((8,)), dma((8,)), dma((8,)), dma((8,)), dma((8,)),
            dma((3, 8)), dma((3, 8)), dma((3, 8)), dma((3, 8)), dma((8,)), dma((2, 4)),
        ],
        compiler_params=pltpu.CompilerParams(
            collective_id=0, has_side_effects=True, vmem_limit_bytes=32 * 1024 * 1024
        ),
        cost_estimate=pl.CostEstimate(flops=1_700_000_000, bytes_accessed=3_000_000, transcendentals=1_500_000),
        name="denoise",
    )(*args)
    outs = jax.ShapeDtypeStruct(x.shape, BF)
    return pl.pallas_call(
        put_out,
        out_shape=(outs, outs),
        in_specs=[vmem] * 2,
        out_specs=(hbm, hbm),
        scratch_shapes=[dma((2,))],
        name="put_out",
    )(*(pltpu.with_memory_space_constraint(z, pltpu.VMEM) for z in (den, eps)))


def solution(mesh):
    clip = P("segment", "frame", "tile", None, None)
    kernel_spec = P("segment", None, None, None, None)
    in_specs = (
        clip, clip, P("segment", "frame"), kernel_spec, kernel_spec, P("segment", None, None, None),
        P("segment", None), P("segment", None, None), P("segment", None, None), kernel_spec, P("segment", None),
    )
    return jax.shard_map(local, mesh=mesh, in_specs=in_specs, out_specs=(clip, clip), check_vma=False)
```

```python
import functools

import jax
import jax.numpy as jnp
from jax import lax
from jax.experimental import pallas as pl
from jax.experimental.pallas import tpu as pltpu
from jax.sharding import PartitionSpec as P

MESH = pl.DeviceIdType.MESH
BF = jnp.bfloat16
F32 = jnp.float32
PR, PC, NF, CH = 4, 16, 16, 128
TR, W = 8, 64
LONG = (0, 1)
DIRS = [(-1, 0), (1, 0), (0, -1), (0, 1), (-1, -1), (-1, 1), (1, -1), (1, 1)]
ROWS, COLS, CORNERS = (0, 1), (2, 3), (4, 5, 6, 7)


def dot(a, b):
    return jnp.dot(a, b, preferred_element_type=F32)


def lane_sums(v, ones):
    hi = v.astype(BF)
    lo = (v - hi.astype(F32)).astype(BF)
    return dot(jnp.concatenate([hi, lo], axis=1), jnp.concatenate([ones, ones], axis=0))


def silu(v):
    half = 0.5 * v
    return half + half * jnp.tanh(half)


def kernel(
    x_hbm, clip_hbm, picks_hbm, w_in, w_mid, proj, factors_hbm, w_up, w_dn, w_out,
    frames_c, xv, v_out,
    picks, factors, raw_n, raw_c, xn, xc, hb, top, bot, lef, rig, acc, res, pk, send_c, zeros, relayed,
    v_in, v_mid, v_proj, v_up, v_dn,
    s_w, s_pk, r_pk, s_c, r_c, s_l, r_n, s_n, s_h, r_h, s_e, r_e, s_o, r_o, s_z, r_l,
):
    s = lax.axis_index("segment")
    t = lax.axis_index("tile")
    d = lax.axis_index("frame")
    i, j = lax.rem(d, 2), lax.div(d, 2)
    big_row = 2 * t + i
    last_tile = lax.axis_size("tile") - 1
    last_row = 2 * last_tile + 1
    last_segment = lax.axis_size("segment") - 1

    def exists(dr, dc):
        row, col = big_row + dr, j + dc
        return (row >= 0) & (row <= last_row) & (col >= 0) & (col <= 3)

    def neighbour(dr, dc):
        row, col = big_row + dr, j + dc
        return {"tile": lax.div(row, 2), "frame": 2 * col + lax.rem(row, 2)}

    def in_group(k):
        return lax.rem(d + k, 8)

    y = 2 * s + lax.rem(t, 2)
    chips = 2 * (last_segment + 1)
    behind, ahead = lax.rem(y + chips - 3, chips), lax.rem(y + 3, chips)
    other_tile = t + 1 - 2 * lax.rem(t, 2)
    relays = (y >= chips - 3) | (y < chips - 5)

    def back_by_three(frame):
        return {"segment": lax.div(behind, 2), "tile": other_tile, "frame": frame}

    def wait_for(ref, sem):
        pltpu.make_async_copy(ref, ref, sem).wait()

    def signal(device):
        pl.semaphore_signal(barrier, inc=1, device_id=device, device_id_type=MESH)

    barrier = pltpu.get_barrier_semaphore()

    @pl.when(s > 0)
    def _():
        for k in range(8):
            if k not in LONG:
                signal({"segment": s - 1, "frame": lax.rem(d + 8 - k, 8)})
        for k in LONG[1:]:
            signal({"segment": lax.div(ahead, 2), "tile": other_tile, "frame": lax.rem(d + 8 - k, 8)})

    signal({"segment": lax.div(ahead, 2), "tile": other_tile})

    for ref in (top, bot, lef, rig):
        ref[...] = jnp.zeros(ref.shape, BF)

    for k in range(1, 8):
        signal({"frame": in_group(k)})

    @pl.when(t > 0)
    def _():
        for q in range(4):
            signal({"tile": t - 1, "frame": 2 * q + 1})

    @pl.when(t < last_tile)
    def _():
        for q in range(4):
            signal({"tile": t + 1, "frame": 2 * q})

    over = t + 2 * i - 1
    over_exists = (over >= 0) & (over <= last_tile)

    weights = [
        (picks_hbm, picks),
        (w_in.at[0], v_in),
        (factors_hbm, factors),
        (w_mid.at[0], v_mid),
        (proj.at[0], v_proj),
        (w_up.at[0], v_up),
        (w_dn.at[0], v_dn),
        (w_out.at[0], v_out),
        (x_hbm.at[0], xv),
    ]
    loads = [pltpu.make_async_copy(a, b, s_w.at[q]) for q, (a, b) in enumerate(weights)]
    for load in loads:
        load.start()
    for buf in (xn, xc, hb):
        buf[0] = jnp.zeros((PC + 2, NF, CH), BF)
        buf[PR + 1] = jnp.zeros((PC + 2, NF, CH), BF)
        buf[:, 0:1] = jnp.zeros((PR + 2, 1, NF, CH), BF)
        buf[:, PC + 1 : PC + 2] = jnp.zeros((PR + 2, 1, NF, CH), BF)
    zeros[...] = jnp.zeros(zeros.shape, BF)

    def no_row(to_row):
        return pltpu.make_async_copy(zeros, frames_c.at[:, to_row : to_row + 1], s_z)

    pl.when(t == 0)(lambda: no_row(0).start())
    pl.when(t == last_tile)(lambda: no_row(TR + 1).start())
    pl.semaphore_wait(barrier, 8 + jnp.where(relays, 1, 0) + jnp.where(s < last_segment, 6, 0) + jnp.where(over_exists, 8, 0))

    def patch_of(ref, c):
        return ref.at[0, :, pl.ds(PR * lax.rem(c, 2), PR), pl.ds(pl.multiple_of(PC * lax.div(c, 2), PC), PC), :]

    def clip_copy(k):
        return pltpu.make_async_remote_copy(
            src_ref=patch_of(clip_hbm, in_group(k)),
            dst_ref=raw_c.at[d],
            send_sem=s_c,
            recv_sem=r_c,
            device_id={"segment": s + 1, "frame": in_group(k)},
            device_id_type=MESH,
        )

    def first_half(q, k):
        return pltpu.make_async_remote_copy(
            src_ref=patch_of(clip_hbm, in_group(k)),
            dst_ref=relayed.at[q],
            send_sem=s_c,
            recv_sem=r_l.at[q],
            device_id=back_by_three(d),
            device_id_type=MESH,
        )

    def second_half(q, k):
        return pltpu.make_async_remote_copy(
            src_ref=relayed.at[q],
            dst_ref=raw_c.at[d],
            send_sem=s_l.at[q],
            recv_sem=r_c,
            device_id=back_by_three(in_group(k)),
            device_id_type=MESH,
        )

    @pl.when(s < last_segment)
    def _():
        for q, k in enumerate(LONG):
            first_half(q, k).start()
        for k in range(8):
            if k not in LONG:
                clip_copy(k).start()

    own_noisy = pltpu.make_async_copy(patch_of(x_hbm, d), raw_n.at[d], s_n.at[0])
    own_noisy.start()
    for k in range(1, 8):
        pltpu.make_async_remote_copy(
            src_ref=patch_of(x_hbm, in_group(k)),
            dst_ref=raw_n.at[d],
            send_sem=s_n.at[1],
            recv_sem=r_n,
            device_id={"frame": in_group(k)},
            device_id_type=MESH,
        ).start()
    loads[0].wait()
    frame_row = lax.broadcasted_iota(jnp.int32, (NF, CH), 0)
    pk[d] = jnp.where(frame_row == 2 * d, picks[0, 0], jnp.where(frame_row == 2 * d + 1, picks[0, 1], 0)).astype(F32)
    for k in range(1, 8):
        pltpu.make_async_remote_copy(
            src_ref=pk.at[d],
            dst_ref=pk.at[d],
            send_sem=s_pk,
            recv_sem=r_pk,
            device_id={"frame": in_group(k)},
            device_id_type=MESH,
        ).start()

    @pl.when(relays)
    def _():
        for q, k in enumerate(LONG):
            first_half(q, k).wait_recv()
            second_half(q, k).start()

    r_i = lax.broadcasted_iota(jnp.int32, (256, 256), 0)
    c_i = lax.broadcasted_iota(jnp.int32, (256, 256), 1)
    r_hi, r_lo, c_hi, c_lo = r_i // 16, r_i % 16, c_i // 16, c_i % 16
    swap = jnp.where((r_hi == c_lo) & (r_lo == c_hi), 1.0, 0.0).astype(BF)

    def halo_copy(buf, n, k):
        inner = slice(1, PC + 1)
        rows = slice(1, PR + 1)
        ends = [
            (buf.at[1, inner], bot.at[n, inner]),
            (buf.at[PR, inner], top.at[n, inner]),
            (buf.at[rows, 1], rig.at[n, rows]),
            (buf.at[rows, PC], lef.at[n, rows]),
            (buf.at[1, 1], bot.at[n, PC + 1]),
            (buf.at[1, PC], bot.at[n, 0]),
            (buf.at[PR, 1], top.at[n, PC + 1]),
            (buf.at[PR, PC], top.at[n, 0]),
        ]
        src, dst = ends[k]
        return pltpu.make_async_remote_copy(
            src_ref=src,
            dst_ref=dst,
            send_sem=s_h.at[k],
            recv_sem=r_h.at[n, k],
            device_id=neighbour(*DIRS[k]),
            device_id_type=MESH,
        )

    def halo_start(buf, n):
        for k in COLS + CORNERS + ROWS:
            pl.when(exists(*DIRS[k]))(halo_copy(buf, n, k).start)

    def halo_wait(buf, n, which):
        for k in which:
            dr, dc = DIRS[k]
            pl.when(exists(-dr, -dc))(halo_copy(buf, n, k).wait_recv)

    def halo_sent(buf, n):
        for k in range(8):
            pl.when(exists(*DIRS[k]))(halo_copy(buf, n, k).wait_send)

    def conv(buf, w, row, rows):
        n = rows * PC * NF
        parts = [
            buf[row + dr : row + dr + rows, dc : dc + PC].reshape(n, CH) for dr in range(3) for dc in range(3)
        ]
        return dot(jnp.concatenate(parts, axis=1), w.reshape(9 * CH, CH)).reshape(rows, PC, NF, CH)

    def add_rows(to, n, w):
        for row, ref, tap in ((0, top, 0), (PR - 1, bot, 2)):
            parts = [ref[n, dc : dc + PC].reshape(PC * NF, CH) for dc in range(3)]
            to[row] += dot(jnp.concatenate(parts, axis=1), w[tap].reshape(3 * CH, CH)).reshape(PC, NF, CH)

    def add_cols(to, n, w):
        for col, ref, tap in ((0, lef, 0), (PC - 1, rig, 2)):
            parts = [ref[n, dr : dr + PR].reshape(PR * NF, CH) for dr in range(3)]
            to[:, col] += dot(jnp.concatenate(parts, axis=1), w[:, tap].reshape(3 * CH, CH)).reshape(PR, NF, CH)

    own_noisy.wait()
    wait_for(raw_n.at[0:7], r_n)
    for row in range(PR):
        xn[row + 1, 1 : PC + 1] = dot(swap, raw_n[:, :, row].reshape(256, CH)).astype(BF).reshape(PC, NF, CH)
    halo_start(xn, 0)
    loads[1].wait()
    for row in (0, 2):
        acc[row : row + 2] = conv(xn, v_in[:, :, 0:CH, :], row, 2)

    wait_for(pk.at[0:7], r_pk)
    pick_rows = pk[0]
    for q in range(1, 8):
        pick_rows = pick_rows + pk[q]
    pick_rows = jnp.broadcast_to(pick_rows[None], (16, NF, CH)).reshape(256, CH)
    pick_rows = jnp.concatenate([pick_rows, pick_rows], axis=1)
    choose = jnp.where((r_hi == c_lo) & (pick_rows == c_hi.astype(F32)), 1.0, 0.0).astype(BF)

    @pl.when(s == 0)
    def _():
        raw_c[...] = jnp.zeros(raw_c.shape, BF)

    @pl.when(s > 0)
    def _():
        wait_for(raw_c, r_c)

    for row in range(PR):
        xc[row + 1, 1 : PC + 1] = dot(choose, raw_c[:, :, row].reshape(256, CH)).astype(BF).reshape(PC, NF, CH)
    halo_sent(xn, 0)
    halo_start(xc, 1)
    for load in loads[2:-2]:
        load.wait()
    for row in (0, 2):
        acc[row : row + 2] += conv(xc, v_in[:, :, CH : 2 * CH, :], row, 2)
    halo_wait(xn, 0, range(8))
    add_rows(acc, 0, v_in[:, :, 0:CH, :])
    add_cols(acc, 0, v_in[:, :, 0:CH, :])
    halo_wait(xc, 1, range(8))
    add_rows(acc, 1, v_in[:, :, CH : 2 * CH, :])
    add_cols(acc, 1, v_in[:, :, CH : 2 * CH, :])
    hb[1 : PR + 1, 1 : PC + 1] = silu(acc[...]).astype(BF)
    halo_sent(xc, 1)
    halo_start(hb, 2)

    lane_r = lax.broadcasted_iota(jnp.int32, (CH, CH), 0)
    lane_c = lax.broadcasted_iota(jnp.int32, (CH, CH), 1)
    ones = jnp.full((CH, CH), 1.0, BF)
    by_head = jnp.where(lane_r // 64 == lane_c // 64, 1.0, 0.0).astype(BF)
    first_head = lane_c < 64
    other_pixel = jnp.where(lane_r // 16 == lane_c // 16, 0.0, -1e30)
    for row in (0, 2):
        skip = hb[row + 1 : row + 3, 1 : PC + 1].astype(F32)
        res[row : row + 2] = skip + conv(hb, v_mid[...], row, 2)

    def two_rows(rows):
        a = jnp.concatenate([res[row].reshape(256, CH) for row in rows], axis=0)
        u = (a * lax.rsqrt(lane_sums(a * a, ones) * (1 / 128) + 1e-6)).astype(BF)
        qkv = dot(u, jnp.concatenate([v_proj[q] for q in range(3)], axis=1))
        q, k, v = qkv[:, 0:CH], qkv[:, CH : 2 * CH], qkv[:, 2 * CH : 3 * CH].astype(BF)
        qn = (q * lax.rsqrt(lane_sums(q * q, by_head) * (1 / 64) + 1e-6)).astype(BF)
        kn = (k * lax.rsqrt(lane_sums(k * k, by_head) * (1 / 64) + 1e-6)).astype(BF)
        parts = []
        zero = jnp.zeros((CH, CH), BF)
        for g in range(4):
            qg, kg, vg = (z[g * CH : (g + 1) * CH] for z in (qn, kn, v))
            both = jnp.concatenate([jnp.where(first_head, qg, zero), jnp.where(first_head, zero, qg)], axis=0)
            sc = lax.dot_general(both, kg, (((1,), (1,)), ((), ())), preferred_element_type=F32)
            sc = jnp.concatenate(
                [sc[h * CH : (h + 1) * CH] * (factors[0, h] * (1 / 64)) + other_pixel for h in range(2)], axis=0
            )
            e = jnp.exp(sc - jnp.max(sc, axis=1, keepdims=True))
            total = jnp.sum(e, axis=1, keepdims=True)
            o = dot(e.astype(BF), vg) / total
            parts.append(jnp.where(first_head, o[:CH], o[CH:]).astype(BF))
        b = a + dot(jnp.concatenate(parts, axis=0), v_proj[3])
        r = (b * lax.rsqrt(lane_sums(b * b, ones) * (1 / 128) + 1e-6)).astype(BF)
        m = silu(dot(r, v_up[...])).astype(BF)
        c = (b + dot(m, v_dn[...])).astype(BF)
        for q, row in enumerate(rows):
            part = dot(swap, c[q * 256 : (q + 1) * 256]).astype(BF)
            send_c[:, row] = part.reshape(NF, PC, CH)

    def give_back(first, size):
        to = frames_c.at[:, pl.ds(1 + PR * i + first, size), pl.ds(pl.multiple_of(PC * j, PC), PC), :]
        for k in range(1, 8):
            pltpu.make_async_remote_copy(
                src_ref=send_c.at[pl.ds(2 * in_group(k), 2), first : first + size],
                dst_ref=to,
                send_sem=s_e.at[0],
                recv_sem=r_e,
                device_id={"frame": in_group(k)},
                device_id_type=MESH,
            ).start()
        pltpu.make_async_copy(send_c.at[pl.ds(2 * d, 2), first : first + size], to, s_e.at[1]).start()

    halo_wait(hb, 2, COLS)
    add_cols(res, 2, v_mid[...])
    halo_wait(hb, 2, ROWS + CORNERS)
    add_rows(res, 2, v_mid[...])
    two_rows((0, 3))

    def over_copy(k, upper):
        first, to_row = (0, TR + 1) if upper else (PR - 1, 0)
        device = {"tile": over, "frame": in_group(k)}
        src = send_c.at[pl.ds(2 * in_group(k), 2), first : first + 1]
        dst = frames_c.at[:, to_row : to_row + 1, pl.ds(pl.multiple_of(PC * j, PC), PC), :]
        return pltpu.make_async_remote_copy(
            src_ref=src,
            dst_ref=dst,
            send_sem=s_o,
            recv_sem=r_o.at[1 if upper else 0],
            device_id=device,
            device_id_type=MESH,
        )

    for upper in (True, False):

        @pl.when(over_exists & (i == (0 if upper else 1)))
        def _(upper=upper):
            for k in range(8):
                over_copy(k, upper).start()

    give_back(0, 1)
    give_back(PR - 1, 1)
    two_rows((1, 2))
    give_back(1, 2)
    halo_sent(hb, 2)
    wait_for(pk.at[0:7], s_pk)
    wait_for(raw_n.at[0:7], s_n.at[1])

    @pl.when(s < last_segment)
    def _():
        wait_for(raw_c, s_c)

    @pl.when(relays)
    def _():
        for q, k in enumerate(LONG):
            second_half(q, k).wait_send()

    pl.when(t == 0)(lambda: no_row(0).wait())
    pl.when(t == last_tile)(lambda: no_row(TR + 1).wait())
    loads[-2].wait()
    loads[-1].wait()
    wait_for(raw_n.at[0:7], s_e.at[0])
    pl.when(over_exists)(lambda: wait_for(send_c.at[:, 0:1], s_o))
    wait_for(raw_n.at[0], s_e.at[1])
    wait_for(raw_n.at[0:7], r_e)
    pl.when(t > 0)(lambda: wait_for(frames_c.at[:, 0:1], r_o.at[0]))
    pl.when(t < last_tile)(lambda: wait_for(frames_c.at[:, TR + 1 : TR + 2], r_o.at[1]))


def last_conv(frames_c, xv, v_out, coefs_hbm, den_out, eps_out, coefs, den, eps, s_in, s_den, s_eps):
    load = pltpu.make_async_copy(coefs_hbm, coefs, s_in)
    load.start()
    column = lax.rem(lax.broadcasted_iota(jnp.int32, (TR * W, CH), 0), W)
    taps = jnp.concatenate([v_out[:, q].reshape(3 * CH, CH) for q in range(3)], axis=1)
    copies = []
    for f in range(2):
        rows = [frames_c[f, dr : dr + TR].reshape(TR * W, CH) for dr in range(3)]
        out = dot(jnp.concatenate(rows, axis=1), taps)
        left = jnp.where(column == 0, 0.0, pltpu.roll(out[:, 0:CH], 1, 0))
        right = jnp.where(column == W - 1, 0.0, pltpu.roll(out[:, 2 * CH :], TR * W - 1, 0))
        total = out[:, CH : 2 * CH] + left + right
        eps[f] = total.astype(BF).reshape(TR, W, CH)
        if f == 0:
            load.wait()
        noisy = xv[f].reshape(TR * W, CH).astype(F32)
        den[f] = (coefs[0, 0] * noisy - coefs[0, 1] * total).astype(BF).reshape(TR, W, CH)
        copies.append(pltpu.make_async_copy(eps.at[f], eps_out.at[0, f], s_eps.at[f]))
        copies.append(pltpu.make_async_copy(den.at[f], den_out.at[0, f], s_den.at[f]))
        copies[-2].start()
        copies[-1].start()
    for copy in copies:
        copy.wait()


def local(x, clip, picks, w_in, w_mid, proj, factors, w_up, w_dn, w_out, coefs):
    args = (x, clip, picks, w_in, w_mid, proj, factors, w_up, w_dn, w_out, coefs)
    args = [pltpu.with_memory_space_constraint(z, pltpu.HBM) for z in args]
    hbm = pl.BlockSpec(memory_space=pltpu.HBM)
    vmem = pl.BlockSpec(memory_space=pltpu.VMEM)
    patch = pltpu.VMEM((8, 2, PR, PC, CH), BF)
    padded = pltpu.VMEM((PR + 2, PC + 2, NF, CH), BF)
    side = pltpu.VMEM((3, PC + 2, NF, CH), BF)
    upright = pltpu.VMEM((3, PR + 2, NF, CH), BF)
    sums = pltpu.VMEM((PR, PC, NF, CH), F32)
    taps = pltpu.VMEM((3, 3, CH, CH), BF)
    dma = pltpu.SemaphoreType.DMA
    frames_c, xv, v_out = pl.pallas_call(
        kernel,
        out_shape=(
            pltpu.VMEM((2, TR + 2, W, CH), BF),
            pltpu.VMEM(x.shape[1:], BF),
            pltpu.VMEM((3, 3, CH, CH), BF),
        ),
        in_specs=[hbm] * 10,
        out_specs=[pl.BlockSpec(memory_space=pl.ANY)] * 3,
        scratch_shapes=[
            pltpu.SMEM((1, 2), jnp.int32),
            pltpu.SMEM((1, 2), F32),
            patch, patch, padded, padded, padded, side, side, upright, upright, sums, sums,
            pltpu.VMEM((8, NF, CH), F32),
            pltpu.VMEM((NF, PR, PC, CH), BF),
            pltpu.VMEM((2, 1, W, CH), BF),
            pltpu.VMEM((2, 2, PR, PC, CH), BF),
            pltpu.VMEM((3, 3, 2 * CH, CH), BF),
            taps,
            pltpu.VMEM((4, CH, CH), BF),
            pltpu.VMEM((CH, 4 * CH), BF),
            pltpu.VMEM((4 * CH, CH), BF),
            dma((9,)), dma, dma, dma, dma, dma((2,)), dma, dma((2,)),
            dma((8,)), dma((3, 8)), dma((2,)), dma, dma, dma((2,)), dma, dma((2,)),
        ],
        compiler_params=pltpu.CompilerParams(
            collective_id=0, has_side_effects=True, vmem_limit_bytes=32 * 1024 * 1024
        ),
        cost_estimate=pl.CostEstimate(flops=1_700_000_000, bytes_accessed=3_000_000, transcendentals=1_500_000),
        name="denoise",
    )(*args[:10])
    outs = jax.ShapeDtypeStruct(x.shape, BF)
    in_vmem = [pltpu.with_memory_space_constraint(z, pltpu.VMEM) for z in (frames_c, xv, v_out)]
    frames = pltpu.VMEM(x.shape[1:], BF)
    return pl.pallas_call(
        last_conv,
        out_shape=(outs, outs),
        in_specs=[vmem, vmem, vmem, hbm],
        out_specs=(hbm, hbm),
        scratch_shapes=[pltpu.SMEM((1, 2), F32), frames, frames, dma, dma((2,)), dma((2,))],
        compiler_params=pltpu.CompilerParams(vmem_limit_bytes=16 * 1024 * 1024),
        name="last_conv",
    )(*in_vmem, args[10])


def solution(mesh):
    clip = P("segment", "frame", "tile", None, None)
    kernel_spec = P("segment", None, None, None, None)
    in_specs = (
        clip, clip, P("segment", "frame"), kernel_spec, kernel_spec, P("segment", None, None, None),
        P("segment", None), P("segment", None, None), P("segment", None, None), kernel_spec, P("segment", None),
    )
    return jax.shard_map(local, mesh=mesh, in_specs=in_specs, out_specs=(clip, clip), check_vma=False)
```

```python
import functools

import jax
import jax.numpy as jnp
from jax import lax
from jax.experimental import pallas as pl
from jax.experimental.pallas import tpu as pltpu
from jax.sharding import PartitionSpec as P

MESH = pl.DeviceIdType.MESH
BF = jnp.bfloat16
F32 = jnp.float32
PR, PC, NF, CH = 4, 16, 16, 128
TR, W = 8, 64
LONG = (0, 1)
DIRS = [(-1, 0), (1, 0), (0, -1), (0, 1), (-1, -1), (-1, 1), (1, -1), (1, 1)]
ROWS, COLS, CORNERS = (0, 1), (2, 3), (4, 5, 6, 7)


def dot(a, b):
    return jnp.dot(a, b, preferred_element_type=F32)


def lane_sums(v, ones):
    hi = v.astype(BF)
    lo = (v - hi.astype(F32)).astype(BF)
    return dot(jnp.concatenate([hi, lo], axis=1), jnp.concatenate([ones, ones], axis=0))


def silu(v):
    half = 0.5 * v
    return half + half * jnp.tanh(half)


def kernel(
    x_hbm, clip_hbm, picks_hbm, w_in, w_mid, proj, factors_hbm, w_up, w_dn, w_out, coefs_hbm,
    frames_c, xv, v_out, coef_rows,
    picks, factors, coefs, coef_block, raw_n, raw_c, xn, xc, hb, top, bot, lef, rig, acc, res, pk, send_c, zeros, relayed,
    v_in, v_mid, v_proj, v_up, v_dn,
    s_w, s_pk, r_pk, s_c, r_c, s_l, r_n, s_n, s_h, r_h, s_e, r_e, s_o, r_o, s_z, r_l,
):
    s = lax.axis_index("segment")
    t = lax.axis_index("tile")
    d = lax.axis_index("frame")
    i, j = lax.rem(d, 2), lax.div(d, 2)
    big_row = 2 * t + i
    last_tile = lax.axis_size("tile") - 1
    last_row = 2 * last_tile + 1
    last_segment = lax.axis_size("segment") - 1

    def exists(dr, dc):
        row, col = big_row + dr, j + dc
        return (row >= 0) & (row <= last_row) & (col >= 0) & (col <= 3)

    def neighbour(dr, dc):
        row, col = big_row + dr, j + dc
        return {"tile": lax.div(row, 2), "frame": 2 * col + lax.rem(row, 2)}

    def in_group(k):
        return lax.rem(d + k, 8)

    y = 2 * s + lax.rem(t, 2)
    chips = 2 * (last_segment + 1)
    behind, ahead = lax.rem(y + chips - 3, chips), lax.rem(y + 3, chips)
    other_tile = t + 1 - 2 * lax.rem(t, 2)
    relays = (y >= chips - 3) | (y < chips - 5)

    def both_round(source):
        return (source != 0) & (source != 3)

    last_source = lax.rem(y + chips - 2, chips)

    def back_by_three(frame):
        return {"segment": lax.div(behind, 2), "tile": other_tile, "frame": frame}

    def wait_for(ref, sem):
        pltpu.make_async_copy(ref, ref, sem).wait()

    def signal(device):
        pl.semaphore_signal(barrier, inc=1, device_id=device, device_id_type=MESH)

    barrier = pltpu.get_barrier_semaphore()

    @pl.when(s > 0)
    def _():
        for k in range(8):
            if k not in LONG:
                signal({"segment": s - 1, "frame": lax.rem(d + 8 - k, 8)})
        sender = lax.rem(d + 8 - LONG[1], 8)

        @pl.when(both_round(last_source))
        def _():
            signal({"segment": lax.div(ahead, 2), "tile": other_tile, "frame": sender})

        @pl.when(jnp.logical_not(both_round(last_source)))
        def _():
            signal({"segment": s - 1, "frame": sender})

    signal({"segment": lax.div(ahead, 2), "tile": other_tile})

    for ref in (top, bot, lef, rig):
        ref[...] = jnp.zeros(ref.shape, BF)

    for k in range(1, 8):
        signal({"frame": in_group(k)})

    @pl.when(t > 0)
    def _():
        for q in range(4):
            signal({"tile": t - 1, "frame": 2 * q + 1})

    @pl.when(t < last_tile)
    def _():
        for q in range(4):
            signal({"tile": t + 1, "frame": 2 * q})

    over = t + 2 * i - 1
    over_exists = (over >= 0) & (over <= last_tile)

    weights = [
        (picks_hbm, picks),
        (w_in.at[0], v_in),
        (factors_hbm, factors),
        (coefs_hbm, coefs),
        (w_mid.at[0], v_mid),
        (proj.at[0], v_proj),
        (w_up.at[0], v_up),
        (w_dn.at[0], v_dn),
        (w_out.at[0], v_out),
        (x_hbm.at[0], xv),
    ]
    loads = [pltpu.make_async_copy(a, b, s_w.at[q]) for q, (a, b) in enumerate(weights)]
    for load in loads:
        load.start()
    for buf in (xn, xc, hb):
        buf[0] = jnp.zeros((PC + 2, NF, CH), BF)
        buf[PR + 1] = jnp.zeros((PC + 2, NF, CH), BF)
        buf[:, 0:1] = jnp.zeros((PR + 2, 1, NF, CH), BF)
        buf[:, PC + 1 : PC + 2] = jnp.zeros((PR + 2, 1, NF, CH), BF)
    zeros[...] = jnp.zeros(zeros.shape, BF)

    def no_row(to_row):
        return pltpu.make_async_copy(zeros, frames_c.at[:, to_row : to_row + 1], s_z.at[0])

    pl.when(t == 0)(lambda: no_row(0).start())
    pl.when(t == last_tile)(lambda: no_row(TR + 1).start())
    pl.semaphore_wait(barrier, 8 + jnp.where(relays & both_round(ahead), 1, 0) + jnp.where(s < last_segment, jnp.where(both_round(y), 6, 7), 0) + jnp.where(over_exists, 8, 0))

    def patch_of(ref, c):
        return ref.at[0, :, pl.ds(PR * lax.rem(c, 2), PR), pl.ds(pl.multiple_of(PC * lax.div(c, 2), PC), PC), :]

    def clip_copy(k):
        return pltpu.make_async_remote_copy(
            src_ref=patch_of(clip_hbm, in_group(k)),
            dst_ref=raw_c.at[d],
            send_sem=s_c,
            recv_sem=r_c,
            device_id={"segment": s + 1, "frame": in_group(k)},
            device_id_type=MESH,
        )

    def first_half(q, k):
        return pltpu.make_async_remote_copy(
            src_ref=patch_of(clip_hbm, in_group(k)),
            dst_ref=relayed.at[q],
            send_sem=s_c,
            recv_sem=r_l.at[q],
            device_id=back_by_three(d),
            device_id_type=MESH,
        )

    def second_half(q, k):
        return pltpu.make_async_remote_copy(
            src_ref=relayed.at[q],
            dst_ref=raw_c.at[d],
            send_sem=s_l.at[q],
            recv_sem=r_c,
            device_id=back_by_three(in_group(k)),
            device_id_type=MESH,
        )

    @pl.when(s < last_segment)
    def _():
        first_half(0, LONG[0]).start()
        pl.when(both_round(y))(lambda: first_half(1, LONG[1]).start())
        pl.when(jnp.logical_not(both_round(y)))(lambda: clip_copy(LONG[1]).start())
        for k in range(8):
            if k not in LONG:
                clip_copy(k).start()

    own_noisy = pltpu.make_async_copy(patch_of(x_hbm, d), raw_n.at[d], s_n.at[0])
    own_noisy.start()
    for k in range(1, 8):
        pltpu.make_async_remote_copy(
            src_ref=patch_of(x_hbm, in_group(k)),
            dst_ref=raw_n.at[d],
            send_sem=s_n.at[1],
            recv_sem=r_n,
            device_id={"frame": in_group(k)},
            device_id_type=MESH,
        ).start()
    loads[0].wait()
    frame_row = lax.broadcasted_iota(jnp.int32, (NF, CH), 0)
    pk[d] = jnp.where(frame_row == 2 * d, picks[0, 0], jnp.where(frame_row == 2 * d + 1, picks[0, 1], 0)).astype(F32)
    for k in range(1, 8):
        pltpu.make_async_remote_copy(
            src_ref=pk.at[d],
            dst_ref=pk.at[d],
            send_sem=s_pk,
            recv_sem=r_pk,
            device_id={"frame": in_group(k)},
            device_id_type=MESH,
        ).start()

    for q, k in enumerate(LONG):

        @pl.when(relays if q == 0 else relays & both_round(ahead))
        def _(q=q, k=k):
            first_half(q, k).wait_recv()
            second_half(q, k).start()

    r_i = lax.broadcasted_iota(jnp.int32, (256, 256), 0)
    c_i = lax.broadcasted_iota(jnp.int32, (256, 256), 1)
    r_hi, r_lo, c_hi, c_lo = r_i // 16, r_i % 16, c_i // 16, c_i % 16
    swap = jnp.where((r_hi == c_lo) & (r_lo == c_hi), 1.0, 0.0).astype(BF)

    def halo_copy(buf, n, k):
        inner = slice(1, PC + 1)
        rows = slice(1, PR + 1)
        ends = [
            (buf.at[1, inner], bot.at[n, inner]),
            (buf.at[PR, inner], top.at[n, inner]),
            (buf.at[rows, 1], rig.at[n, rows]),
            (buf.at[rows, PC], lef.at[n, rows]),
            (buf.at[1, 1], bot.at[n, PC + 1]),
            (buf.at[1, PC], bot.at[n, 0]),
            (buf.at[PR, 1], top.at[n, PC + 1]),
            (buf.at[PR, PC], top.at[n, 0]),
        ]
        src, dst = ends[k]
        return pltpu.make_async_remote_copy(
            src_ref=src,
            dst_ref=dst,
            send_sem=s_h.at[n % 2, k],
            recv_sem=r_h.at[n, k],
            device_id=neighbour(*DIRS[k]),
            device_id_type=MESH,
        )

    def halo_start(buf, n):
        for k in COLS + CORNERS + ROWS:
            pl.when(exists(*DIRS[k]))(halo_copy(buf, n, k).start)

    def halo_wait(buf, n, which):
        for k in which:
            dr, dc = DIRS[k]
            pl.when(exists(-dr, -dc))(halo_copy(buf, n, k).wait_recv)

    def halo_sent(buf, n):
        for k in range(8):
            pl.when(exists(*DIRS[k]))(halo_copy(buf, n, k).wait_send)

    def conv(buf, w, row, rows):
        n = rows * PC * NF
        parts = [
            buf[row + dr : row + dr + rows, dc : dc + PC].reshape(n, CH) for dr in range(3) for dc in range(3)
        ]
        return dot(jnp.concatenate(parts, axis=1), w.reshape(9 * CH, CH)).reshape(rows, PC, NF, CH)

    def add_rows(to, n, w):
        for row, ref, tap in ((0, top, 0), (PR - 1, bot, 2)):
            parts = [ref[n, dc : dc + PC].reshape(PC * NF, CH) for dc in range(3)]
            to[row] += dot(jnp.concatenate(parts, axis=1), w[tap].reshape(3 * CH, CH)).reshape(PC, NF, CH)

    def add_cols(to, n, w):
        for col, ref, tap in ((0, lef, 0), (PC - 1, rig, 2)):
            parts = [ref[n, dr : dr + PR].reshape(PR * NF, CH) for dr in range(3)]
            to[:, col] += dot(jnp.concatenate(parts, axis=1), w[:, tap].reshape(3 * CH, CH)).reshape(PR, NF, CH)

    own_noisy.wait()
    wait_for(raw_n.at[0:7], r_n)
    for row in range(PR):
        xn[row + 1, 1 : PC + 1] = dot(swap, raw_n[:, :, row].reshape(256, CH)).astype(BF).reshape(PC, NF, CH)
    halo_start(xn, 0)
    loads[1].wait()
    for row in (0, 2):
        acc[row : row + 2] = conv(xn, v_in[:, :, 0:CH, :], row, 2)

    wait_for(pk.at[0:7], r_pk)
    pick_rows = pk[0]
    for q in range(1, 8):
        pick_rows = pick_rows + pk[q]
    pick_rows = jnp.broadcast_to(pick_rows[None], (16, NF, CH)).reshape(256, CH)
    pick_rows = jnp.concatenate([pick_rows, pick_rows], axis=1)
    choose = jnp.where((r_hi == c_lo) & (pick_rows == c_hi.astype(F32)), 1.0, 0.0).astype(BF)

    @pl.when(s == 0)
    def _():
        raw_c[...] = jnp.zeros(raw_c.shape, BF)

    @pl.when(s > 0)
    def _():
        wait_for(raw_c, r_c)

    for row in range(PR):
        xc[row + 1, 1 : PC + 1] = dot(choose, raw_c[:, :, row].reshape(256, CH)).astype(BF).reshape(PC, NF, CH)
    halo_start(xc, 1)
    for load in loads[2:-2]:
        load.wait()
    half_row = lax.broadcasted_iota(jnp.int32, (8, CH), 0) < 4
    coef_block[...] = jnp.where(half_row, coefs[0, 0], coefs[0, 1])
    coef_copy = pltpu.make_async_copy(coef_block, coef_rows, s_z.at[1])
    coef_copy.start()
    for row in (0, 2):
        acc[row : row + 2] += conv(xc, v_in[:, :, CH : 2 * CH, :], row, 2)
    halo_wait(xn, 0, range(8))
    add_rows(acc, 0, v_in[:, :, 0:CH, :])
    add_cols(acc, 0, v_in[:, :, 0:CH, :])
    halo_wait(xc, 1, range(8))
    add_rows(acc, 1, v_in[:, :, CH : 2 * CH, :])
    add_cols(acc, 1, v_in[:, :, CH : 2 * CH, :])
    hb[1 : PR + 1, 1 : PC + 1] = silu(acc[...]).astype(BF)
    halo_sent(xn, 0)
    halo_start(hb, 2)

    lane_r = lax.broadcasted_iota(jnp.int32, (CH, CH), 0)
    lane_c = lax.broadcasted_iota(jnp.int32, (CH, CH), 1)
    ones = jnp.full((CH, CH), 1.0, BF)
    by_head = jnp.where(lane_r // 64 == lane_c // 64, 1.0, 0.0).astype(BF)
    first_head = lane_c < 64
    other_pixel = jnp.where(lane_r // 16 == lane_c // 16, 0.0, -1e30)
    for row in (0, 2):
        skip = hb[row + 1 : row + 3, 1 : PC + 1].astype(F32)
        res[row : row + 2] = skip + conv(hb, v_mid[...], row, 2)

    def two_rows(rows):
        a = jnp.concatenate([res[row].reshape(256, CH) for row in rows], axis=0)
        u = (a * lax.rsqrt(jnp.mean(a * a, axis=1, keepdims=True) + 1e-6)).astype(BF)
        qkv = dot(u, jnp.concatenate([v_proj[q] for q in range(3)], axis=1))
        q, k, v = qkv[:, 0:CH], qkv[:, CH : 2 * CH], qkv[:, 2 * CH : 3 * CH].astype(BF)
        qn = (q * lax.rsqrt(lane_sums(q * q, by_head) * (1 / 64) + 1e-6)).astype(BF)
        kn = (k * lax.rsqrt(lane_sums(k * k, by_head) * (1 / 64) + 1e-6)).astype(BF)
        parts = []
        zero = jnp.zeros((CH, CH), BF)
        for g in range(4):
            qg, kg, vg = (z[g * CH : (g + 1) * CH] for z in (qn, kn, v))
            both = jnp.concatenate([jnp.where(first_head, qg, zero), jnp.where(first_head, zero, qg)], axis=0)
            sc = lax.dot_general(both, kg, (((1,), (1,)), ((), ())), preferred_element_type=F32)
            sc = jnp.concatenate(
                [sc[h * CH : (h + 1) * CH] * (factors[0, h] * (1 / 64)) + other_pixel for h in range(2)], axis=0
            )
            e = jnp.exp(sc - jnp.max(sc, axis=1, keepdims=True))
            total = jnp.sum(e, axis=1, keepdims=True)
            o = dot(e.astype(BF), vg)
            total = jnp.where(first_head, total[:CH], total[CH:])
            parts.append((jnp.where(first_head, o[:CH], o[CH:]) / total).astype(BF))
        b = a + dot(jnp.concatenate(parts, axis=0), v_proj[3])
        r = (b * lax.rsqrt(jnp.mean(b * b, axis=1, keepdims=True) + 1e-6)).astype(BF)
        m = silu(dot(r, v_up[...])).astype(BF)
        c = (b + dot(m, v_dn[...])).astype(BF)
        for q, row in enumerate(rows):
            part = dot(swap, c[q * 256 : (q + 1) * 256]).astype(BF)
            send_c[:, row] = part.reshape(NF, PC, CH)

    def give_back(first, size):
        to = frames_c.at[:, pl.ds(1 + PR * i + first, size), pl.ds(pl.multiple_of(PC * j, PC), PC), :]
        for k in range(1, 8):
            pltpu.make_async_remote_copy(
                src_ref=send_c.at[pl.ds(2 * in_group(k), 2), first : first + size],
                dst_ref=to,
                send_sem=s_e.at[0],
                recv_sem=r_e,
                device_id={"frame": in_group(k)},
                device_id_type=MESH,
            ).start()
        pltpu.make_async_copy(send_c.at[pl.ds(2 * d, 2), first : first + size], to, s_e.at[1]).start()

    halo_wait(hb, 2, COLS)
    add_cols(res, 2, v_mid[...])
    halo_wait(hb, 2, ROWS + CORNERS)
    add_rows(res, 2, v_mid[...])
    two_rows((0, 3))

    def over_copy(k, upper):
        first, to_row = (0, TR + 1) if upper else (PR - 1, 0)
        device = {"tile": over, "frame": in_group(k)}
        src = send_c.at[pl.ds(2 * in_group(k), 2), first : first + 1]
        dst = frames_c.at[:, to_row : to_row + 1, pl.ds(pl.multiple_of(PC * j, PC), PC), :]
        return pltpu.make_async_remote_copy(
            src_ref=src,
            dst_ref=dst,
            send_sem=s_o,
            recv_sem=r_o.at[1 if upper else 0],
            device_id=device,
            device_id_type=MESH,
        )

    for upper in (True, False):

        @pl.when(over_exists & (i == (0 if upper else 1)))
        def _(upper=upper):
            for k in range(8):
                over_copy(k, upper).start()

    give_back(0, 1)
    give_back(PR - 1, 1)
    two_rows((1, 2))
    give_back(1, 2)
    halo_sent(xc, 1)
    halo_sent(hb, 2)
    wait_for(pk.at[0:7], s_pk)
    wait_for(raw_n.at[0:7], s_n.at[1])

    @pl.when(s < last_segment)
    def _():
        wait_for(raw_c, s_c)

    for q, k in enumerate(LONG):

        @pl.when(relays if q == 0 else relays & both_round(ahead))
        def _(q=q, k=k):
            second_half(q, k).wait_send()

    pl.when(t == 0)(lambda: no_row(0).wait())
    pl.when(t == last_tile)(lambda: no_row(TR + 1).wait())
    coef_copy.wait()
    loads[-2].wait()
    loads[-1].wait()
    wait_for(raw_n.at[0:7], s_e.at[0])
    pl.when(over_exists)(lambda: wait_for(send_c.at[:, 0:1], s_o))
    wait_for(raw_n.at[0], s_e.at[1])
    wait_for(raw_n.at[0:7], r_e)
    pl.when(t > 0)(lambda: wait_for(frames_c.at[:, 0:1], r_o.at[0]))
    pl.when(t < last_tile)(lambda: wait_for(frames_c.at[:, TR + 1 : TR + 2], r_o.at[1]))


def last_conv(frames_c, xv, v_out, coef_rows, den_out, eps_out, den, eps, s_den, s_eps):
    column = lax.rem(lax.broadcasted_iota(jnp.int32, (TR * W, CH), 0), W)
    taps = jnp.concatenate([v_out[:, q].reshape(3 * CH, CH) for q in range(3)], axis=1)
    copies = []
    for f in range(2):
        rows = [frames_c[f, dr : dr + TR].reshape(TR * W, CH) for dr in range(3)]
        out = dot(jnp.concatenate(rows, axis=1), taps)
        left = jnp.where(column == 0, 0.0, pltpu.roll(out[:, 0:CH], 1, 0))
        right = jnp.where(column == W - 1, 0.0, pltpu.roll(out[:, 2 * CH :], TR * W - 1, 0))
        total = out[:, CH : 2 * CH] + left + right
        eps[f] = total.astype(BF).reshape(TR, W, CH)
        copies.append(pltpu.make_async_copy(eps.at[f], eps_out.at[0, f], s_eps.at[f]))
        copies[-1].start()
        noisy = xv[f].reshape(TR * W, CH).astype(F32)
        den[f] = (coef_rows[0:1] * noisy - coef_rows[4:5] * total).astype(BF).reshape(TR, W, CH)
        copies.append(pltpu.make_async_copy(den.at[f], den_out.at[0, f], s_den.at[f]))
        copies[-1].start()
    for copy in copies:
        copy.wait()


def local(x, clip, picks, w_in, w_mid, proj, factors, w_up, w_dn, w_out, coefs):
    args = (x, clip, picks, w_in, w_mid, proj, factors, w_up, w_dn, w_out, coefs)
    args = [pltpu.with_memory_space_constraint(z, pltpu.HBM) for z in args]
    hbm = pl.BlockSpec(memory_space=pltpu.HBM)
    vmem = pl.BlockSpec(memory_space=pltpu.VMEM)
    patch = pltpu.VMEM((8, 2, PR, PC, CH), BF)
    padded = pltpu.VMEM((PR + 2, PC + 2, NF, CH), BF)
    side = pltpu.VMEM((3, PC + 2, NF, CH), BF)
    upright = pltpu.VMEM((3, PR + 2, NF, CH), BF)
    sums = pltpu.VMEM((PR, PC, NF, CH), F32)
    taps = pltpu.VMEM((3, 3, CH, CH), BF)
    dma = pltpu.SemaphoreType.DMA
    frames_c, xv, v_out, coef_rows = pl.pallas_call(
        kernel,
        out_shape=(
            pltpu.VMEM((2, TR + 2, W, CH), BF),
            pltpu.VMEM(x.shape[1:], BF),
            pltpu.VMEM((3, 3, CH, CH), BF),
            pltpu.VMEM((8, CH), F32),
        ),
        in_specs=[hbm] * 11,
        out_specs=[pl.BlockSpec(memory_space=pl.ANY)] * 4,
        scratch_shapes=[
            pltpu.SMEM((1, 2), jnp.int32),
            pltpu.SMEM((1, 2), F32),
            pltpu.SMEM((1, 2), F32),
            pltpu.VMEM((8, CH), F32),
            patch, patch, padded, padded, padded, side, side, upright, upright, sums, sums,
            pltpu.VMEM((8, NF, CH), F32),
            pltpu.VMEM((NF, PR, PC, CH), BF),
            pltpu.VMEM((2, 1, W, CH), BF),
            pltpu.VMEM((2, 2, PR, PC, CH), BF),
            pltpu.VMEM((3, 3, 2 * CH, CH), BF),
            taps,
            pltpu.VMEM((4, CH, CH), BF),
            pltpu.VMEM((CH, 4 * CH), BF),
            pltpu.VMEM((4 * CH, CH), BF),
            dma((10,)), dma, dma, dma, dma, dma((2,)), dma, dma((2,)),
            dma((2, 8)), dma((3, 8)), dma((2,)), dma, dma, dma((2,)), dma((2,)), dma((2,)),
        ],
        compiler_params=pltpu.CompilerParams(
            collective_id=0, has_side_effects=True, vmem_limit_bytes=32 * 1024 * 1024
        ),
        cost_estimate=pl.CostEstimate(flops=1_700_000_000, bytes_accessed=3_000_000, transcendentals=1_500_000),
        name="denoise",
    )(*args)
    outs = jax.ShapeDtypeStruct(x.shape, BF)
    in_vmem = [pltpu.with_memory_space_constraint(z, pltpu.VMEM) for z in (frames_c, xv, v_out, coef_rows)]
    frames = pltpu.VMEM(x.shape[1:], BF)
    return pl.pallas_call(
        last_conv,
        out_shape=(outs, outs),
        in_specs=[vmem] * 4,
        out_specs=(hbm, hbm),
        scratch_shapes=[frames, frames, dma((2,)), dma((2,))],
        compiler_params=pltpu.CompilerParams(vmem_limit_bytes=16 * 1024 * 1024),
        name="last_conv",
    )(*in_vmem)


def solution(mesh):
    clip = P("segment", "frame", "tile", None, None)
    kernel_spec = P("segment", None, None, None, None)
    in_specs = (
        clip, clip, P("segment", "frame"), kernel_spec, kernel_spec, P("segment", None, None, None),
        P("segment", None), P("segment", None, None), P("segment", None, None), kernel_spec, P("segment", None),
    )
    return jax.shard_map(local, mesh=mesh, in_specs=in_specs, out_specs=(clip, clip), check_vma=False)
```

```python
import functools

import jax
import jax.numpy as jnp
from jax import lax
from jax.experimental import pallas as pl
from jax.experimental.pallas import tpu as pltpu
from jax.sharding import PartitionSpec as P

MESH = pl.DeviceIdType.MESH
BF = jnp.bfloat16
F32 = jnp.float32
PR, PC, NF, CH = 4, 16, 16, 128
TR, W = 8, 64
LONG = (0, 1)
DIRS = [(-1, 0), (1, 0), (0, -1), (0, 1), (-1, -1), (-1, 1), (1, -1), (1, 1)]
ROWS, COLS, CORNERS = (0, 1), (2, 3), (4, 5, 6, 7)


def dot(a, b):
    return jnp.dot(a, b, preferred_element_type=F32)


def lane_sums(v, ones):
    hi = v.astype(BF)
    lo = (v - hi.astype(F32)).astype(BF)
    return dot(jnp.concatenate([hi, lo], axis=1), jnp.concatenate([ones, ones], axis=0))


def silu(v):
    half = 0.5 * v
    return half + half * jnp.tanh(half)


def kernel(
    x_hbm, clip_hbm, picks_hbm, w_in, w_mid, proj, factors_hbm, w_up, w_dn, w_out, coefs_hbm,
    frames_c, xv, v_out, coef_rows,
    picks, factors, coefs, coef_block, raw_n, raw_c, xn, xc, hb, top, bot, lef, rig, acc, res, pk, send_c, zeros, relayed,
    v_in, v_mid, v_proj, v_up, v_dn,
    s_w, s_pk, r_pk, s_c, r_c, s_l, r_n, s_n, s_h, r_h, s_e, r_e, s_o, r_o, s_z, r_l,
):
    s = lax.axis_index("segment")
    t = lax.axis_index("tile")
    d = lax.axis_index("frame")
    i, j = lax.rem(d, 2), lax.div(d, 2)
    big_row = 2 * t + i
    last_tile = lax.axis_size("tile") - 1
    last_row = 2 * last_tile + 1
    last_segment = lax.axis_size("segment") - 1

    def exists(dr, dc):
        row, col = big_row + dr, j + dc
        return (row >= 0) & (row <= last_row) & (col >= 0) & (col <= 3)

    def neighbour(dr, dc):
        row, col = big_row + dr, j + dc
        return {"tile": lax.div(row, 2), "frame": 2 * col + lax.rem(row, 2)}

    def in_group(k):
        return lax.rem(d + k, 8)

    y = 2 * s + lax.rem(t, 2)
    chips = 2 * (last_segment + 1)
    behind, ahead = lax.rem(y + chips - 3, chips), lax.rem(y + 3, chips)
    other_tile = t + 1 - 2 * lax.rem(t, 2)
    relays = (y >= chips - 3) | (y < chips - 5)

    def both_round(source):
        return (source != 0) & (source != 3)

    last_source = lax.rem(y + chips - 2, chips)

    def back_by_three(frame):
        return {"segment": lax.div(behind, 2), "tile": other_tile, "frame": frame}

    def wait_for(ref, sem):
        pltpu.make_async_copy(ref, ref, sem).wait()

    def signal(device):
        pl.semaphore_signal(barrier, inc=1, device_id=device, device_id_type=MESH)

    barrier = pltpu.get_barrier_semaphore()

    @pl.when(s > 0)
    def _():
        for k in range(8):
            if k not in LONG:
                signal({"segment": s - 1, "frame": lax.rem(d + 8 - k, 8)})
        sender = lax.rem(d + 8 - LONG[1], 8)

        @pl.when(both_round(last_source))
        def _():
            signal({"segment": lax.div(ahead, 2), "tile": other_tile, "frame": sender})

        @pl.when(jnp.logical_not(both_round(last_source)))
        def _():
            signal({"segment": s - 1, "frame": sender})

    signal({"segment": lax.div(ahead, 2), "tile": other_tile})

    for ref in (top, bot, lef, rig):
        ref[...] = jnp.zeros(ref.shape, BF)

    for k in range(1, 8):
        signal({"frame": in_group(k)})

    @pl.when(t > 0)
    def _():
        for q in range(4):
            signal({"tile": t - 1, "frame": 2 * q + 1})

    @pl.when(t < last_tile)
    def _():
        for q in range(4):
            signal({"tile": t + 1, "frame": 2 * q})

    over = t + 2 * i - 1
    over_exists = (over >= 0) & (over <= last_tile)

    weights = [
        (picks_hbm, picks),
        (w_in.at[0], v_in),
        (factors_hbm, factors),
        (coefs_hbm, coefs),
        (w_mid.at[0], v_mid),
        (proj.at[0], v_proj),
        (w_up.at[0], v_up),
        (w_dn.at[0], v_dn),
        (w_out.at[0], v_out),
        (x_hbm.at[0], xv),
    ]
    loads = [pltpu.make_async_copy(a, b, s_w.at[q]) for q, (a, b) in enumerate(weights)]
    for load in loads:
        load.start()
    for buf in (xn, xc, hb):
        buf[0] = jnp.zeros((PC + 2, NF, CH), BF)
        buf[PR + 1] = jnp.zeros((PC + 2, NF, CH), BF)
        buf[:, 0:1] = jnp.zeros((PR + 2, 1, NF, CH), BF)
        buf[:, PC + 1 : PC + 2] = jnp.zeros((PR + 2, 1, NF, CH), BF)
    zeros[...] = jnp.zeros(zeros.shape, BF)

    def no_row(to_row):
        return pltpu.make_async_copy(zeros, frames_c.at[:, to_row : to_row + 1], s_z.at[0])

    pl.when(t == 0)(lambda: no_row(0).start())
    pl.when(t == last_tile)(lambda: no_row(TR + 1).start())
    pl.semaphore_wait(barrier, 8 + jnp.where(relays & both_round(ahead), 1, 0) + jnp.where(s < last_segment, jnp.where(both_round(y), 6, 7), 0) + jnp.where(over_exists, 8, 0))

    def patch_of(ref, c):
        return ref.at[0, :, pl.ds(PR * lax.rem(c, 2), PR), pl.ds(pl.multiple_of(PC * lax.div(c, 2), PC), PC), :]

    def clip_copy(k):
        return pltpu.make_async_remote_copy(
            src_ref=patch_of(clip_hbm, in_group(k)),
            dst_ref=raw_c.at[d],
            send_sem=s_c,
            recv_sem=r_c,
            device_id={"segment": s + 1, "frame": in_group(k)},
            device_id_type=MESH,
        )

    def first_half(q, k):
        return pltpu.make_async_remote_copy(
            src_ref=patch_of(clip_hbm, in_group(k)),
            dst_ref=relayed.at[q],
            send_sem=s_c,
            recv_sem=r_l.at[q],
            device_id=back_by_three(d),
            device_id_type=MESH,
        )

    def second_half(q, k):
        return pltpu.make_async_remote_copy(
            src_ref=relayed.at[q],
            dst_ref=raw_c.at[d],
            send_sem=s_l.at[q],
            recv_sem=r_c,
            device_id=back_by_three(in_group(k)),
            device_id_type=MESH,
        )

    @pl.when(s < last_segment)
    def _():
        first_half(0, LONG[0]).start()
        pl.when(both_round(y))(lambda: first_half(1, LONG[1]).start())
        pl.when(jnp.logical_not(both_round(y)))(lambda: clip_copy(LONG[1]).start())
        for k in range(8):
            if k not in LONG:
                clip_copy(k).start()

    own_noisy = pltpu.make_async_copy(patch_of(x_hbm, d), raw_n.at[d], s_n.at[0])
    own_noisy.start()
    for k in range(1, 8):
        pltpu.make_async_remote_copy(
            src_ref=patch_of(x_hbm, in_group(k)),
            dst_ref=raw_n.at[d],
            send_sem=s_n.at[1],
            recv_sem=r_n,
            device_id={"frame": in_group(k)},
            device_id_type=MESH,
        ).start()
    loads[0].wait()
    frame_row = lax.broadcasted_iota(jnp.int32, (NF, CH), 0)
    pk[d] = jnp.where(frame_row == 2 * d, picks[0, 0], jnp.where(frame_row == 2 * d + 1, picks[0, 1], 0)).astype(F32)
    for k in range(1, 8):
        pltpu.make_async_remote_copy(
            src_ref=pk.at[d],
            dst_ref=pk.at[d],
            send_sem=s_pk,
            recv_sem=r_pk,
            device_id={"frame": in_group(k)},
            device_id_type=MESH,
        ).start()

    for q, k in enumerate(LONG):

        @pl.when(relays if q == 0 else relays & both_round(ahead))
        def _(q=q, k=k):
            first_half(q, k).wait_recv()
            second_half(q, k).start()

    r_i = lax.broadcasted_iota(jnp.int32, (256, 256), 0)
    c_i = lax.broadcasted_iota(jnp.int32, (256, 256), 1)
    r_hi, r_lo, c_hi, c_lo = r_i // 16, r_i % 16, c_i // 16, c_i % 16
    swap = jnp.where((r_hi == c_lo) & (r_lo == c_hi), 1.0, 0.0).astype(BF)

    def halo_copy(buf, n, k):
        inner = slice(1, PC + 1)
        rows = slice(1, PR + 1)
        ends = [
            (buf.at[1, inner], bot.at[n, inner]),
            (buf.at[PR, inner], top.at[n, inner]),
            (buf.at[rows, 1], rig.at[n, rows]),
            (buf.at[rows, PC], lef.at[n, rows]),
            (buf.at[1, 1], bot.at[n, PC + 1]),
            (buf.at[1, PC], bot.at[n, 0]),
            (buf.at[PR, 1], top.at[n, PC + 1]),
            (buf.at[PR, PC], top.at[n, 0]),
        ]
        src, dst = ends[k]
        return pltpu.make_async_remote_copy(
            src_ref=src,
            dst_ref=dst,
            send_sem=s_h.at[n % 2, k],
            recv_sem=r_h.at[n, k],
            device_id=neighbour(*DIRS[k]),
            device_id_type=MESH,
        )

    def halo_start(buf, n):
        for k in COLS + CORNERS:
            pl.when(exists(*DIRS[k]))(halo_copy(buf, n, k).start)
        pl.when(exists(*DIRS[0]) & (i == 0))(halo_copy(buf, n, 0).start)
        pl.when(exists(*DIRS[1]))(halo_copy(buf, n, 1).start)
        pl.when(exists(*DIRS[0]) & (i == 1))(halo_copy(buf, n, 0).start)

    def halo_wait(buf, n, which):
        for k in which:
            dr, dc = DIRS[k]
            pl.when(exists(-dr, -dc))(halo_copy(buf, n, k).wait_recv)

    def halo_sent(buf, n):
        for k in range(8):
            pl.when(exists(*DIRS[k]))(halo_copy(buf, n, k).wait_send)

    def conv(buf, w, row, rows):
        n = rows * PC * NF
        parts = [
            buf[row + dr : row + dr + rows, dc : dc + PC].reshape(n, CH) for dr in range(3) for dc in range(3)
        ]
        return dot(jnp.concatenate(parts, axis=1), w.reshape(9 * CH, CH)).reshape(rows, PC, NF, CH)

    def add_rows(to, n, w):
        for row, ref, tap in ((0, top, 0), (PR - 1, bot, 2)):
            parts = [ref[n, dc : dc + PC].reshape(PC * NF, CH) for dc in range(3)]
            to[row] += dot(jnp.concatenate(parts, axis=1), w[tap].reshape(3 * CH, CH)).reshape(PC, NF, CH)

    def add_cols(to, n, w):
        for col, ref, tap in ((0, lef, 0), (PC - 1, rig, 2)):
            parts = [ref[n, dr : dr + PR].reshape(PR * NF, CH) for dr in range(3)]
            to[:, col] += dot(jnp.concatenate(parts, axis=1), w[:, tap].reshape(3 * CH, CH)).reshape(PR, NF, CH)

    own_noisy.wait()
    wait_for(raw_n.at[0:7], r_n)
    for row in range(PR):
        xn[row + 1, 1 : PC + 1] = dot(swap, raw_n[:, :, row].reshape(256, CH)).astype(BF).reshape(PC, NF, CH)
    halo_start(xn, 0)
    loads[1].wait()
    for row in (0, 2):
        acc[row : row + 2] = conv(xn, v_in[:, :, 0:CH, :], row, 2)

    wait_for(pk.at[0:7], r_pk)
    pick_rows = pk[0]
    for q in range(1, 8):
        pick_rows = pick_rows + pk[q]
    pick_rows = jnp.broadcast_to(pick_rows[None], (16, NF, CH)).reshape(256, CH)
    pick_rows = jnp.concatenate([pick_rows, pick_rows], axis=1)
    choose = jnp.where((r_hi == c_lo) & (pick_rows == c_hi.astype(F32)), 1.0, 0.0).astype(BF)

    @pl.when(s == 0)
    def _():
        raw_c[...] = jnp.zeros(raw_c.shape, BF)

    @pl.when(s > 0)
    def _():
        wait_for(raw_c, r_c)

    for row in range(PR):
        xc[row + 1, 1 : PC + 1] = dot(choose, raw_c[:, :, row].reshape(256, CH)).astype(BF).reshape(PC, NF, CH)
    halo_start(xc, 1)
    for load in loads[2:-2]:
        load.wait()
    half_row = lax.broadcasted_iota(jnp.int32, (8, CH), 0) < 4
    coef_block[...] = jnp.where(half_row, coefs[0, 0], coefs[0, 1])
    coef_copy = pltpu.make_async_copy(coef_block, coef_rows, s_z.at[1])
    coef_copy.start()
    for row in (0, 2):
        acc[row : row + 2] += conv(xc, v_in[:, :, CH : 2 * CH, :], row, 2)
    halo_wait(xn, 0, range(8))
    add_rows(acc, 0, v_in[:, :, 0:CH, :])
    add_cols(acc, 0, v_in[:, :, 0:CH, :])
    halo_wait(xc, 1, COLS)
    add_cols(acc, 1, v_in[:, :, CH : 2 * CH, :])
    halo_wait(xc, 1, ROWS + CORNERS)
    add_rows(acc, 1, v_in[:, :, CH : 2 * CH, :])
    hb[1 : PR + 1, 1 : PC + 1] = silu(acc[...]).astype(BF)
    halo_sent(xn, 0)
    halo_start(hb, 2)

    lane_r = lax.broadcasted_iota(jnp.int32, (CH, CH), 0)
    lane_c = lax.broadcasted_iota(jnp.int32, (CH, CH), 1)
    ones = jnp.full((CH, CH), 1.0, BF)
    by_head = jnp.where(lane_r // 64 == lane_c // 64, 1.0, 0.0).astype(BF)
    first_head = lane_c < 64
    other_pixel = jnp.where(lane_r // 16 == lane_c // 16, 0.0, -1e30)
    for row in (0, 2):
        skip = hb[row + 1 : row + 3, 1 : PC + 1].astype(F32)
        res[row : row + 2] = skip + conv(hb, v_mid[...], row, 2)

    def two_rows(rows):
        a = jnp.concatenate([res[row].reshape(256, CH) for row in rows], axis=0)
        u = (a * lax.rsqrt(jnp.mean(a * a, axis=1, keepdims=True) + 1e-6)).astype(BF)
        qkv = dot(u, jnp.concatenate([v_proj[q] for q in range(3)], axis=1))
        q, k, v = qkv[:, 0:CH], qkv[:, CH : 2 * CH], qkv[:, 2 * CH : 3 * CH].astype(BF)
        qn = (q * lax.rsqrt(lane_sums(q * q, by_head) * (1 / 64) + 1e-6)).astype(BF)
        kn = (k * lax.rsqrt(lane_sums(k * k, by_head) * (1 / 64) + 1e-6)).astype(BF)
        parts = []
        zero = jnp.zeros((CH, CH), BF)
        for g in range(4):
            qg, kg, vg = (z[g * CH : (g + 1) * CH] for z in (qn, kn, v))
            both = jnp.concatenate([jnp.where(first_head, qg, zero), jnp.where(first_head, zero, qg)], axis=0)
            sc = lax.dot_general(both, kg, (((1,), (1,)), ((), ())), preferred_element_type=F32)
            sc = jnp.concatenate(
                [sc[h * CH : (h + 1) * CH] * (factors[0, h] * (1 / 64)) + other_pixel for h in range(2)], axis=0
            )
            e = jnp.exp(sc - jnp.max(sc, axis=1, keepdims=True))
            total = jnp.sum(e, axis=1, keepdims=True)
            o = dot(e.astype(BF), vg)
            total = jnp.where(first_head, total[:CH], total[CH:])
            parts.append((jnp.where(first_head, o[:CH], o[CH:]) / total).astype(BF))
        b = a + dot(jnp.concatenate(parts, axis=0), v_proj[3])
        r = (b * lax.rsqrt(jnp.mean(b * b, axis=1, keepdims=True) + 1e-6)).astype(BF)
        m = silu(dot(r, v_up[...])).astype(BF)
        c = (b + dot(m, v_dn[...])).astype(BF)
        for q, row in enumerate(rows):
            part = dot(swap, c[q * 256 : (q + 1) * 256]).astype(BF)
            send_c[:, row] = part.reshape(NF, PC, CH)

    def give_back(first, size):
        to = frames_c.at[:, pl.ds(1 + PR * i + first, size), pl.ds(pl.multiple_of(PC * j, PC), PC), :]
        for k in range(1, 8):
            pltpu.make_async_remote_copy(
                src_ref=send_c.at[pl.ds(2 * in_group(k), 2), first : first + size],
                dst_ref=to,
                send_sem=s_e.at[0],
                recv_sem=r_e,
                device_id={"frame": in_group(k)},
                device_id_type=MESH,
            ).start()
        pltpu.make_async_copy(send_c.at[pl.ds(2 * d, 2), first : first + size], to, s_e.at[1]).start()

    halo_wait(hb, 2, COLS)
    add_cols(res, 2, v_mid[...])
    halo_wait(hb, 2, ROWS + CORNERS)
    add_rows(res, 2, v_mid[...])
    two_rows((0, 3))

    def over_copy(k, upper):
        first, to_row = (0, TR + 1) if upper else (PR - 1, 0)
        device = {"tile": over, "frame": in_group(k)}
        src = send_c.at[pl.ds(2 * in_group(k), 2), first : first + 1]
        dst = frames_c.at[:, to_row : to_row + 1, pl.ds(pl.multiple_of(PC * j, PC), PC), :]
        return pltpu.make_async_remote_copy(
            src_ref=src,
            dst_ref=dst,
            send_sem=s_o,
            recv_sem=r_o.at[1 if upper else 0],
            device_id=device,
            device_id_type=MESH,
        )

    for upper in (True, False):

        @pl.when(over_exists & (i == (0 if upper else 1)))
        def _(upper=upper):
            for k in range(8):
                over_copy(k, upper).start()

    give_back(0, 1)
    give_back(PR - 1, 1)
    two_rows((1, 2))
    give_back(1, 2)
    halo_sent(xc, 1)
    halo_sent(hb, 2)
    wait_for(pk.at[0:7], s_pk)
    wait_for(raw_n.at[0:7], s_n.at[1])

    @pl.when(s < last_segment)
    def _():
        wait_for(raw_c, s_c)

    for q, k in enumerate(LONG):

        @pl.when(relays if q == 0 else relays & both_round(ahead))
        def _(q=q, k=k):
            second_half(q, k).wait_send()

    pl.when(t == 0)(lambda: no_row(0).wait())
    pl.when(t == last_tile)(lambda: no_row(TR + 1).wait())
    coef_copy.wait()
    loads[-2].wait()
    loads[-1].wait()
    wait_for(raw_n.at[0:7], s_e.at[0])
    pl.when(over_exists)(lambda: wait_for(send_c.at[:, 0:1], s_o))
    wait_for(raw_n.at[0], s_e.at[1])
    wait_for(raw_n.at[0:7], r_e)
    pl.when(t > 0)(lambda: wait_for(frames_c.at[:, 0:1], r_o.at[0]))
    pl.when(t < last_tile)(lambda: wait_for(frames_c.at[:, TR + 1 : TR + 2], r_o.at[1]))


def last_conv(frames_c, xv, v_out, coef_rows, den_out, eps_out, den, eps, s_den, s_eps):
    column = lax.rem(lax.broadcasted_iota(jnp.int32, (TR * W, CH), 0), W)
    taps = jnp.concatenate([v_out[:, q].reshape(3 * CH, CH) for q in range(3)], axis=1)
    copies = []
    for f in range(2):
        rows = [frames_c[f, dr : dr + TR].reshape(TR * W, CH) for dr in range(3)]
        out = dot(jnp.concatenate(rows, axis=1), taps)
        left = jnp.where(column == 0, 0.0, pltpu.roll(out[:, 0:CH], 1, 0))
        right = jnp.where(column == W - 1, 0.0, pltpu.roll(out[:, 2 * CH :], TR * W - 1, 0))
        total = out[:, CH : 2 * CH] + left + right
        eps[f] = total.astype(BF).reshape(TR, W, CH)
        copies.append(pltpu.make_async_copy(eps.at[f], eps_out.at[0, f], s_eps.at[f]))
        copies[-1].start()
        noisy = xv[f].reshape(TR * W, CH).astype(F32)
        den[f] = (coef_rows[0:1] * noisy - coef_rows[4:5] * total).astype(BF).reshape(TR, W, CH)
        copies.append(pltpu.make_async_copy(den.at[f], den_out.at[0, f], s_den.at[f]))
        copies[-1].start()
    for copy in copies:
        copy.wait()


def local(x, clip, picks, w_in, w_mid, proj, factors, w_up, w_dn, w_out, coefs):
    args = (x, clip, picks, w_in, w_mid, proj, factors, w_up, w_dn, w_out, coefs)
    args = [pltpu.with_memory_space_constraint(z, pltpu.HBM) for z in args]
    hbm = pl.BlockSpec(memory_space=pltpu.HBM)
    vmem = pl.BlockSpec(memory_space=pltpu.VMEM)
    patch = pltpu.VMEM((8, 2, PR, PC, CH), BF)
    padded = pltpu.VMEM((PR + 2, PC + 2, NF, CH), BF)
    side = pltpu.VMEM((3, PC + 2, NF, CH), BF)
    upright = pltpu.VMEM((3, PR + 2, NF, CH), BF)
    sums = pltpu.VMEM((PR, PC, NF, CH), F32)
    taps = pltpu.VMEM((3, 3, CH, CH), BF)
    dma = pltpu.SemaphoreType.DMA
    frames_c, xv, v_out, coef_rows = pl.pallas_call(
        kernel,
        out_shape=(
            pltpu.VMEM((2, TR + 2, W, CH), BF),
            pltpu.VMEM(x.shape[1:], BF),
            pltpu.VMEM((3, 3, CH, CH), BF),
            pltpu.VMEM((8, CH), F32),
        ),
        in_specs=[hbm] * 11,
        out_specs=[pl.BlockSpec(memory_space=pl.ANY)] * 4,
        scratch_shapes=[
            pltpu.SMEM((1, 2), jnp.int32),
            pltpu.SMEM((1, 2), F32),
            pltpu.SMEM((1, 2), F32),
            pltpu.VMEM((8, CH), F32),
            patch, patch, padded, padded, padded, side, side, upright, upright, sums, sums,
            pltpu.VMEM((8, NF, CH), F32),
            pltpu.VMEM((NF, PR, PC, CH), BF),
            pltpu.VMEM((2, 1, W, CH), BF),
            pltpu.VMEM((2, 2, PR, PC, CH), BF),
            pltpu.VMEM((3, 3, 2 * CH, CH), BF),
            taps,
            pltpu.VMEM((4, CH, CH), BF),
            pltpu.VMEM((CH, 4 * CH), BF),
            pltpu.VMEM((4 * CH, CH), BF),
            dma((10,)), dma, dma, dma, dma, dma((2,)), dma, dma((2,)),
            dma((2, 8)), dma((3, 8)), dma((2,)), dma, dma, dma((2,)), dma((2,)), dma((2,)),
        ],
        compiler_params=pltpu.CompilerParams(
            collective_id=0, has_side_effects=True, vmem_limit_bytes=32 * 1024 * 1024
        ),
        cost_estimate=pl.CostEstimate(flops=1_700_000_000, bytes_accessed=3_000_000, transcendentals=1_500_000),
        name="denoise",
    )(*args)
    outs = jax.ShapeDtypeStruct(x.shape, BF)
    in_vmem = [pltpu.with_memory_space_constraint(z, pltpu.VMEM) for z in (frames_c, xv, v_out, coef_rows)]
    frames = pltpu.VMEM(x.shape[1:], BF)
    return pl.pallas_call(
        last_conv,
        out_shape=(outs, outs),
        in_specs=[vmem] * 4,
        out_specs=(hbm, hbm),
        scratch_shapes=[frames, frames, dma((2,)), dma((2,))],
        compiler_params=pltpu.CompilerParams(vmem_limit_bytes=16 * 1024 * 1024),
        name="last_conv",
    )(*in_vmem)


def solution(mesh):
    clip = P("segment", "frame", "tile", None, None)
    kernel_spec = P("segment", None, None, None, None)
    in_specs = (
        clip, clip, P("segment", "frame"), kernel_spec, kernel_spec, P("segment", None, None, None),
        P("segment", None), P("segment", None, None), P("segment", None, None), kernel_spec, P("segment", None),
    )
    return jax.shard_map(local, mesh=mesh, in_specs=in_specs, out_specs=(clip, clip), check_vma=False)
```
